32 devices in a mesh: space: 8 (over y, x, core), slot: 4 (over z).
Axes of the slice: x: 2, y: 2, z: 4, core: 2. Of those that a mesh axis runs over, the one named last changes fastest.
Arguments:
- window_values: bfloat16 [16384, 8192], P('space', 'slot'), may hold values from -4 to 4
- window_scales: bfloat16 [128, 8192], P('space', 'slot'), may hold values from 0.049804688 to 1
- slab_values: bfloat16 [16384, 512], P('space', 'slot'), may hold values from -4 to 4
- slab_scales: bfloat16 [128, 512], P('space', 'slot'), may hold values from 0.049804688 to 1
- test_matrix: bfloat16 [8192, 256], P('slot'), may hold values from -1 to 1
- owner_slot: int32 [4], replicated, may hold values from 0 to 3, each once
- offset: int32 [1], replicated, may hold values from 0 to 1536
Outputs:
- pod_basis: bfloat16 [16384, 256], P('space')
- pod_coefs: float32 [256, 8192], P(None, 'slot')
The draws below stay inside these ranges and needn't reach their ends.
All inputs are finite; a program needn't handle non-finite values.
Results may differ from the reference program's by a relative error of at most 0.0049.
Values may be sent and summed in bfloat16 or wider, within the bound.
A program may use at most 128 MiB of HBM per device.

```python
import math
import jax
import jax.numpy as jnp
from jax import lax

ROWS_DEV = 2048
COLS_DEV = 2048
RANK = 256
SLAB = 512
BLOCK = 128
ROWS = 16384
COLS = 8192
N_SPACE = 8
N_SLOT = 4


def snapshot_values(key, row_count, col_count):
    entries = jax.random.normal(jax.random.fold_in(key, 13), (row_count, col_count), jnp.float32)
    return jnp.clip(entries, -4.0, 4.0).astype(jnp.bfloat16)


def draw_window_values(key, part):
    return snapshot_values(key, ROWS, COLS)


def draw_slab_values(key, part):
    return snapshot_values(key, ROWS, SLAB)


def draw_test_matrix(key, part):
    entries = jnp.clip(jax.random.normal(jax.random.fold_in(key, 22), (COLS, RANK), jnp.float32), -6.0, 6.0)
    return (entries / jnp.sqrt(jnp.float32(COLS))).astype(jnp.bfloat16)


def levels(own_key, shape, cuts, smallest, largest):
    level, own = 1.0, jax.random.fold_in(own_key, 6)
    for position, shards_of in cuts:
        draws = jnp.exp(jax.random.uniform(jax.random.fold_in(own, position), (shards_of,), jnp.float32, smallest / len(cuts), largest / len(cuts)))
        level = level * jnp.repeat(draws, shape[position] // shards_of).reshape([-1 if axis == position else 1 for axis in range(len(shape))])
    return level


def setup_inputs(seed: int = 0) -> dict:
    key_list = jax.random.split(jax.random.key(seed), 8)
    return {
        "window_values": draw_window_values(jax.random.fold_in(key_list[7], 71), 0),
        "window_scales": jnp.clip(jnp.exp(math.log(1.0) - 2.9996462 * jax.random.uniform(key_list[1], (ROWS // BLOCK, COLS), jnp.float32) ** levels(key_list[1], (ROWS // BLOCK, COLS), ((0, 8), (1, 4)), -0.2, 0.2)), 0.049804688, 1.0).astype(jnp.bfloat16),
        "slab_values": draw_slab_values(jax.random.fold_in(key_list[7], 71), 0),
        "slab_scales": jnp.clip(jnp.exp(math.log(1.0) - 2.9996462 * jax.random.uniform(key_list[3], (ROWS // BLOCK, SLAB), jnp.float32) ** levels(key_list[3], (ROWS // BLOCK, SLAB), ((0, 8), (1, 4)), -0.2, 0.2)), 0.049804688, 1.0).astype(jnp.bfloat16),
        "test_matrix": draw_test_matrix(jax.random.fold_in(key_list[7], 71), 0),
        "owner_slot": jax.random.permutation(key_list[5], N_SLOT).astype(jnp.int32),
        "offset": jax.random.randint(key_list[6], (1,), 0, COLS_DEV - SLAB + 1).astype(jnp.int32),
    }


def expand(values, scales):
    row_count, col_count = values.shape
    scaled = values.astype(jnp.float32).reshape(row_count // BLOCK, BLOCK, col_count) * scales.astype(jnp.float32)[:, None, :]
    return scaled.reshape(row_count, col_count).astype(jnp.bfloat16)

def inverse_factor(gram_matrix):
    lower_factor = jnp.linalg.cholesky(gram_matrix)
    identity = jnp.eye(gram_matrix.shape[0], dtype=jnp.float32)
    return lax.linalg.triangular_solve(lower_factor, identity, left_side=True, lower=True)

def reference(window_values, window_scales, slab_values, slab_scales, test_matrix, owner_slot, offset):
    first_col = (owner_slot[0] * COLS_DEV + offset[0]).astype(jnp.int32)
    values = lax.dynamic_update_slice(window_values, slab_values, (jnp.int32(0), first_col))
    scales = lax.dynamic_update_slice(window_scales, slab_scales, (jnp.int32(0), first_col))
    value_blocks = values.reshape(N_SPACE, ROWS_DEV, COLS)
    scale_blocks = scales.reshape(N_SPACE, ROWS_DEV // BLOCK, COLS)

    def sketch_block(blocks):
        return jnp.dot(expand(blocks[0], blocks[1]).astype(jnp.float32), test_matrix.astype(jnp.float32), preferred_element_type=jnp.float32)
    sketch = lax.map(sketch_block, (value_blocks, scale_blocks))
    flat_sketch = sketch.reshape(ROWS, RANK)
    gram_matrix = jnp.dot(flat_sketch.T.astype(jnp.float32), flat_sketch.astype(jnp.float32), precision=lax.Precision.HIGHEST, preferred_element_type=jnp.float32) / ROWS
    inverse = inverse_factor(gram_matrix)
    pod_basis = jnp.dot(flat_sketch.astype(jnp.float32), inverse.T.astype(jnp.float32), precision=lax.Precision.HIGHEST, preferred_element_type=jnp.float32).astype(jnp.bfloat16)

    def cross_block(accum_sum, blocks):
        window = expand(blocks[0], blocks[1]).astype(jnp.float32)
        partial_value = lax.dot_general(blocks[2].astype(jnp.float32), window.astype(jnp.float32), (((0,), (0,)), ((), ())), precision=lax.Precision.HIGHEST, preferred_element_type=jnp.float32)
        return (accum_sum + partial_value, None)
    cross, _ = lax.scan(cross_block, jnp.zeros((RANK, COLS), jnp.float32), (value_blocks, scale_blocks, sketch))
    pod_coefs = jnp.dot(inverse.astype(jnp.float32), cross.astype(jnp.float32), precision=lax.Precision.HIGHEST, preferred_element_type=jnp.float32)
    return (pod_basis, pod_coefs / jnp.sqrt(jnp.float32(ROWS)))
```

```python
import functools

import jax
import jax.numpy as jnp
from jax import lax
from jax.experimental import pallas as pl
from jax.experimental.pallas import tpu as pltpu
from jax.sharding import PartitionSpec as P

MESH = pl.DeviceIdType.MESH
F32, BF16 = jnp.float32, jnp.bfloat16
SUB = 2


def dot(a, b, contract=((1,), (0,))):
    return lax.dot_general(a, b, (contract, ((), ())), preferred_element_type=F32)


def dot_full(a, b, contract=((1,), (0,))):
    return lax.dot_general(
        a, b, (contract, ((), ())), precision=lax.Precision.HIGHEST, preferred_element_type=F32
    )


def split(x):
    hi = x.astype(BF16)
    return hi, (x - hi.astype(F32)).astype(BF16)


def inverse_lower(t_ref, size, between):
    row = lax.broadcasted_iota(jnp.int32, (size, size), 0)
    lane = lax.broadcasted_iota(jnp.int32, (size, size), 1)
    sub8 = lax.broadcasted_iota(jnp.int32, (8, size), 0)
    lane8 = lax.broadcasted_iota(jnp.int32, (8, size), 1)
    lane1 = lax.broadcasted_iota(jnp.int32, (1, size), 1)

    def round_of(g, _):
        t = t_ref[...]
        tile = t_ref[pl.ds(pl.multiple_of(g * 8, 8), 8), :]
        for s in range(8):
            below = row > g * 8 + s
            below8 = sub8 > s
            r = tile[s : s + 1, :]
            inv = 1.0 / tile[s : s + 1, s : s + 1]
            r = jnp.where(lane1 == s, 1.0, r) * inv
            col8 = jnp.where(below8, tile[:, s : s + 1], 0.0)
            tile = jnp.where(below8 & (lane8 == s), 0.0, tile) - col8 * r
            col = jnp.where(below, t[:, s : s + 1], 0.0)
            t = jnp.where(below & (lane == s), 0.0, t) - col * r
        t_ref[...] = pltpu.roll(t, size - 8, 1)
        return 0

    rounds = size // 8
    parts = len(between) + 1
    edges = [rounds * i // parts for i in range(parts + 1)]
    for i in range(parts):
        lax.fori_loop(edges[i], edges[i + 1], round_of, 0)
        if i < len(between):
            between[i]()
    t = t_ref[...]
    pivot = jnp.sum(jnp.where(row == lane, t, 0.0), axis=1, keepdims=True)
    unit = jnp.where(row > lane, t, jnp.where(row == lane, 1.0, 0.0))
    return unit * lax.rsqrt(pivot)


def kernel(
    n, nsp,
    vals, scales, slab, slab_sc, test, owner, offset,
    basis_o, coef_o,
    win, win_s, msc, place, tm_out, tm_in, part, rs_out, rs_in, sk, skt,
    gr, g_out, g_in, g_fin, cr, c_out, c_in, c_fin, sl_in, t_ref, inv_ref,
    tm_ss, tm_rs, rr_ss, rr_rs, rl_ss, rl_rs, ar_ss, ar_rs, al_ss, al_rs,
    g_ss, g_rs, c_ss, c_rs, sl_ss, sl_rs,
):
    z = lax.axis_index("slot")
    me = lax.axis_index("space")
    core = lax.rem(me, 2)
    rows, cols = vals.shape
    rank = test.shape[1]
    block = rows // scales.shape[0]
    sc = slab.shape[1]
    sw = sl_in.shape[2]
    nb = nsp.bit_length() - 1
    half = rank // 2
    chunk = rows // n
    sub = chunk // SUB
    total_rows = rows * nsp

    strides = [jnp.int32(1)]
    for i in range(1, nb):
        strides.append((1 << i) * (1 - core) + (1 << (nb - i)) * core)
    strides.append(jnp.int32(1))

    def partner(stride):
        return me + stride * (1 - 2 * lax.rem(me // stride, 2))

    def copy(src, dst, ss, rs, space=None, slot=None):
        return pltpu.make_async_remote_copy(
            src_ref=src, dst_ref=dst, send_sem=ss, recv_sem=rs,
            device_id={"space": me if space is None else space, "slot": z if slot is None else slot},
            device_id_type=MESH,
        )

    barrier = pltpu.get_barrier_semaphore()
    for d in range(1, n):
        pl.semaphore_signal(
            barrier, inc=1, device_id={"space": me, "slot": lax.rem(z + d, n)}, device_id_type=MESH
        )
    for i in range(nb):
        pl.semaphore_signal(
            barrier, inc=1, device_id={"space": partner(jnp.int32(1 << i)), "slot": z}, device_id_type=MESH
        )

    first = jnp.where(owner[0] == z, offset[0], -(2 ** 20))

    @pl.loop(0, n)
    def _(s):
        diff = lax.broadcasted_iota(jnp.int32, (sc, cols), 1) - lax.broadcasted_iota(
            jnp.int32, (sc, cols), 0
        )
        one_hot = jnp.where(diff == first + s * sc, 1.0, 0.0).astype(BF16)
        place[pl.ds(pl.multiple_of(s * sc, sc), sc), :] = one_hot
        tm_out[s] = dot(one_hot, test[...]).astype(BF16)

    pl.semaphore_wait(barrier, n - 1 + nb)

    def tm_copy(d):
        peer = lax.rem(z + d, n)
        return copy(tm_out.at[peer], tm_in.at[d], tm_ss.at[d], tm_rs.at[d], slot=peer)

    for d in range(1, n):
        tm_copy(d).start()

    col = lax.broadcasted_iota(jnp.int32, scales.shape, 1) - first
    replaced = (col >= 0) & (col < n * sc)
    msc[...] = jnp.where(replaced, 0.0, scales[...].astype(F32))

    ssc = slab_sc[...].astype(F32)
    for b in range(rows // block):
        win_s[b * block : (b + 1) * block, :] = (
            slab[b * block : (b + 1) * block, :].astype(F32) * ssc[b : b + 1, :]
        ).astype(BF16)

    @pl.loop(0, rows // block)
    def _(b):
        at = pl.ds(pl.multiple_of(b * block, block), block)
        w = (vals[at, :].astype(F32) * msc[pl.ds(b, 1), :]).astype(BF16)
        win[at, :] = w
        part[at, :] = dot(w, test[...])

    rows_new = tm_out[z].astype(F32)
    for d in range(1, n):
        tm_copy(d).wait_recv()
        rows_new += tm_in[d].astype(F32)
    rows_new = rows_new.astype(BF16)

    @pl.loop(0, n)
    def _(c):
        at = pl.ds(pl.multiple_of(c * chunk, chunk), chunk)
        part[at, :] += dot(win_s[at, :], rows_new)

    def span(c, h):
        return pl.ds(pl.multiple_of(c * chunk + h * sub, sub), sub)

    def rs_copy(way, c, h):
        ss, rs = ((rr_ss, rr_rs), (rl_ss, rl_rs))[way]
        step = 1 - 2 * way
        at = span(c, h)
        return copy(
            rs_out.at[way, at], rs_in.at[way, at], ss.at[c, h], rs.at[c, h], slot=z + step
        )

    has = (z > 0, z < n - 1)
    for d in range(n - 1, 0, -1):
        for h in range(SUB):
            for way in (0, 1):
                c = z + d * (1 - 2 * way)

                @pl.when((c >= 0) & (c < n))
                def _():
                    at = span(c, h)

                    @pl.when(has[way])
                    def _():
                        rs_copy(way, c, h).wait_recv()
                        part[at, :] += rs_in[way, at, :].astype(F32)

                    rs_out[way, at, :] = part[at, :].astype(BF16)
                    rs_copy(way, c, h).start()

    def ag_copy(way, c, h):
        ss, rs = ((ar_ss, ar_rs), (al_ss, al_rs))[way]
        at = span(c, h)
        return copy(sk.at[at], sk.at[at], ss.at[c, h], rs.at[c, h], slot=z + 1 - 2 * way)

    for h in range(SUB):
        at = span(z, h)
        for way in (0, 1):

            @pl.when(has[way])
            def _():
                rs_copy(way, z, h).wait_recv()
                part[at, :] += rs_in[way, at, :].astype(F32)

        sk[at, :] = part[at, :].astype(BF16)
        for way in (0, 1):

            @pl.when(has[1 - way])
            def _():
                ag_copy(way, z, h).start()

    for d in range(1, n):
        for h in range(SUB):
            for way in (0, 1):
                c = z - d * (1 - 2 * way)

                @pl.when((c >= 0) & (c < n))
                def _():
                    ag_copy(way, c, h).wait_recv()

                    @pl.when(has[1 - way])
                    def _():
                        ag_copy(way, c, h).start()

    @pl.loop(0, n)
    def _(c):
        at = pl.ds(pl.multiple_of(c * chunk, chunk), chunk)
        skt[:, at] = sk[at, :].astype(F32).T.astype(BF16)

    def half_at(c):
        return pl.ds(pl.multiple_of(c * half, half), half)

    def g_copy(i):
        if i == 0:
            return copy(gr.at[half_at(1 - core)], g_in.at[0], g_ss.at[0], g_rs.at[0], space=partner(strides[0]))
        if i < nb:
            return copy(g_out.at[i], g_in.at[i], g_ss.at[i], g_rs.at[i], space=partner(strides[i]))
        at = half_at(core)
        return copy(g_fin.at[at], g_fin.at[at], g_ss.at[i], g_rs.at[i], space=partner(strides[0]))

    def g_step(i):
        own = gr[half_at(core), :] if i == 1 else g_out[i - 1]
        g_copy(i - 1).wait_recv()
        total = own + g_in[i - 1]
        if i < nb:
            g_out[i] = total
        else:
            g_fin[half_at(core), :] = total
        g_copy(i).start()

    gr[...] = dot(skt[...], sk[...])
    g_copy(0).start()

    width = 2 * rank if cols % (2 * rank) == 0 else rank
    blocks = cols // width
    cr[:, cols:] = jnp.zeros((rank, sw), F32)
    cr[:, cols : cols + sc] = dot(skt[...], win_s[...])
    for i in range(nb):

        @pl.loop(blocks * i // nb, blocks * (i + 1) // nb)
        def _(b):
            at = pl.ds(pl.multiple_of(b * width, width), width)
            cr[:, at] = dot(skt[...], win[:, at])

        if i + 1 < nb:
            g_step(i + 1)

    def c_copy(i):
        if i < nb:
            return copy(c_out.at[i], c_in.at[i], c_ss.at[i], c_rs.at[i], space=partner(strides[i]))
        at = half_at(core)
        return copy(c_fin.at[at], c_fin.at[at], c_ss.at[i], c_rs.at[i], space=partner(strides[0]))

    c_out[0] = cr[half_at(1 - core), :].astype(BF16)
    c_copy(0).start()

    def c_step(i):
        c_copy(i - 1).wait_recv()
        own = cr[half_at(core), :] if i == 1 else c_out[i - 1].astype(F32)
        total = (own + c_in[i - 1].astype(F32)).astype(BF16)
        if i < nb:
            c_out[i] = total
        else:
            c_fin[half_at(core), :] = total
        c_copy(i).start()

    def sl_copy(d):
        return copy(
            c_fin.at[:, pl.ds(cols, sw)], sl_in.at[d], sl_ss.at[d], sl_rs.at[d], slot=lax.rem(z + d, n)
        )

    def sl_start():
        c_copy(nb).wait_recv()
        for d in range(1, n):
            sl_copy(d).start()

    g_step(nb)
    c_step(1)
    g_copy(nb).wait_recv()

    steps = [functools.partial(c_step, i) for i in range(2, nb + 1)] + [sl_start]
    cut = (len(steps) + 1) // 2
    scale = 1.0 / total_rows
    t_ref[...] = g_fin[:half, :half] * scale
    inv1 = inverse_lower(t_ref, half, steps[:cut])
    low = dot_full(g_fin[half:, :half] * scale, inv1, ((1,), (1,)))
    t_ref[...] = g_fin[half:, half:] * scale - dot_full(low, low, ((1,), (1,)))
    inv2 = inverse_lower(t_ref, half, steps[cut:])
    inv_ref[:half, :half] = inv1
    inv_ref[:half, half:] = jnp.zeros((half, half), F32)
    inv_ref[half:, :half] = -dot_full(inv2, dot_full(low, inv1))
    inv_ref[half:, half:] = inv2

    hi, lo = split(inv_ref[...])

    @pl.loop(0, n)
    def _(c):
        at = pl.ds(pl.multiple_of(c * chunk, chunk), chunk)
        s = sk[at, :]
        basis_o[at, :] = (dot(s, hi, ((1,), (1,))) + dot(s, lo, ((1,), (1,)))).astype(BF16)

    for d in range(1, n):
        sl_copy(d).wait_recv()
    norm = 1.0 / (total_rows ** 0.5)

    @pl.loop(0, blocks)
    def _(b):
        at = pl.ds(pl.multiple_of(b * width, width), width)
        x = c_fin[:, at].astype(F32)
        for d in range(n):
            src = lax.rem(z + n - d, n)
            p = place[pl.ds(pl.multiple_of(src * sc, sc), sc), at]
            own = c_fin[:, cols : cols + sc] if d == 0 else sl_in[d, :, :sc]
            x += dot(own, p)
        x = x.astype(BF16)
        coef_o[:, at] = (dot(hi, x) + dot(lo, x)) * norm

    for d in range(1, n):
        tm_copy(d).wait_send()
        sl_copy(d).wait_send()
        for h in range(SUB):
            for way in (0, 1):
                c = z + d * (1 - 2 * way)

                @pl.when((c >= 0) & (c < n))
                def _():
                    rs_copy(way, c, h).wait_send()

    for d in range(n):
        for h in range(SUB):
            for way in (0, 1):
                c = z - d * (1 - 2 * way)

                @pl.when((c >= 0) & (c < n) & has[1 - way])
                def _():
                    ag_copy(way, c, h).wait_send()

    for i in range(nb + 1):
        g_copy(i).wait_send()
        c_copy(i).wait_send()


def local(n, nsp, vals, scales, slab, slab_sc, test, owner, offset):
    rows, cols = vals.shape
    rank = test.shape[1]
    sc = slab.shape[1]
    sw = -(-sc // 128) * 128
    nb = nsp.bit_length() - 1
    half = rank // 2
    vmem = pl.BlockSpec(memory_space=pltpu.VMEM)
    smem = pl.BlockSpec(memory_space=pltpu.SMEM)
    dma = pltpu.SemaphoreType.DMA
    flops = 2 * rank * (2 * rows * cols + 3 * rank * rows + 2 * rank * cols)
    return pl.pallas_call(
        functools.partial(kernel, n, nsp),
        out_shape=(
            jax.ShapeDtypeStruct((rows, rank), BF16),
            jax.ShapeDtypeStruct((rank, cols), F32),
        ),
        in_specs=[vmem] * 5 + [smem] * 2,
        out_specs=(vmem, vmem),
        scratch_shapes=[
            pltpu.VMEM((rows, cols), BF16),
            pltpu.VMEM((rows, sc), BF16),
            pltpu.VMEM(scales.shape, F32),
            pltpu.VMEM((n * sc, cols), BF16),
            pltpu.VMEM((n, sc, rank), BF16),
            pltpu.VMEM((n, sc, rank), BF16),
            pltpu.VMEM((rows, rank), F32),
            pltpu.VMEM((2, rows, rank), BF16),
            pltpu.VMEM((2, rows, rank), BF16),
            pltpu.VMEM((rows, rank), BF16),
            pltpu.VMEM((rank, rows), BF16),
            pltpu.VMEM((rank, rank), F32),
            pltpu.VMEM((nb, half, rank), F32),
            pltpu.VMEM((nb, half, rank), F32),
            pltpu.VMEM((rank, rank), F32),
            pltpu.VMEM((rank, cols + sw), F32),
            pltpu.VMEM((nb, half, cols + sw), BF16),
            pltpu.VMEM((nb, half, cols + sw), BF16),
            pltpu.VMEM((rank, cols + sw), BF16),
            pltpu.VMEM((n, rank, sw), BF16),
            pltpu.VMEM((half, half), F32),
            pltpu.VMEM((rank, rank), F32),
            dma((n,)), dma((n,)),
            dma((n, SUB)), dma((n, SUB)), dma((n, SUB)), dma((n, SUB)),
            dma((n, SUB)), dma((n, SUB)), dma((n, SUB)), dma((n, SUB)),
            dma((nb + 1,)), dma((nb + 1,)), dma((nb + 1,)), dma((nb + 1,)),
            dma((n,)), dma((n,)),
        ],
        compiler_params=pltpu.CompilerParams(
            collective_id=0, has_side_effects=True, vmem_limit_bytes=60 * 2 ** 20
        ),
        cost_estimate=pl.CostEstimate(
            flops=flops, bytes_accessed=2 * rows * cols + 4 * rank * cols, transcendentals=0
        ),
    )(vals, scales, slab, slab_sc, test, owner, offset)


def solution(mesh):
    return jax.shard_map(
        functools.partial(local, mesh.shape["slot"], mesh.shape["space"]),
        mesh=mesh,
        in_specs=(
            P("space", "slot"),
            P("space", "slot"),
            P("space", "slot"),
            P("space", "slot"),
            P("slot", None),
            P(),
            P(),
        ),
        out_specs=(P("space", None), P(None, "slot")),
        check_vma=False,
    )
```

```python
import functools

import jax
import jax.numpy as jnp
from jax import lax
from jax.experimental import pallas as pl
from jax.experimental.pallas import tpu as pltpu
from jax.sharding import PartitionSpec as P

MESH = pl.DeviceIdType.MESH
F32, BF16 = jnp.float32, jnp.bfloat16
SUB = 2


def dot(a, b, contract=((1,), (0,))):
    return lax.dot_general(a, b, (contract, ((), ())), preferred_element_type=F32)


def dot_full(a, b, contract=((1,), (0,))):
    return lax.dot_general(
        a, b, (contract, ((), ())), precision=lax.Precision.HIGHEST, preferred_element_type=F32
    )


def split(x):
    hi = x.astype(BF16)
    return hi, (x - hi.astype(F32)).astype(BF16)


def inverse_lower(t_ref, size, between):
    row = lax.broadcasted_iota(jnp.int32, (size, size), 0)
    lane = lax.broadcasted_iota(jnp.int32, (size, size), 1)
    sub8 = lax.broadcasted_iota(jnp.int32, (8, size), 0)
    lane8 = lax.broadcasted_iota(jnp.int32, (8, size), 1)
    lane1 = lax.broadcasted_iota(jnp.int32, (1, size), 1)

    def round_of(g, _):
        rest = t_ref[8:, :]
        tile = t_ref[:8, :]
        cols = [jnp.broadcast_to(tile[:, j : j + 1], (8, size)) for j in range(8)]
        inv8 = jnp.zeros((8, size), F32)
        for s in range(8):
            inv = 1.0 / cols[s][s : s + 1, :]
            inv8 = jnp.where(sub8 == s, inv, inv8)
            m = jnp.where(sub8 > s, cols[s] * inv, 0.0)
            r = jnp.where(lane1 == s, 1.0, tile[s : s + 1, :])
            for j in range(s + 1, 8):
                cols[j] = cols[j] - m * cols[j][s : s + 1, :]
            tile = jnp.where((sub8 > s) & (lane8 == s), 0.0, tile) - m * r
        left = size - 8 * g
        mult = jnp.where((lane8 >= 8) & (lane8 < left), tile * inv8, 0.0)
        unit = jnp.where(lane8 < sub8, tile, jnp.where(lane8 == sub8, 1.0, 0.0))
        rows = jnp.where(lane8 < 8, unit, tile)
        change = dot_full(mult, rows, ((0,), (0,)))
        open_rows = (row[8:] < left) & (lane[8:] < 8)
        rest = jnp.where(open_rows, 0.0, rest) - change[8:]
        t_ref[: size - 8, :] = pltpu.roll(rest, size - 8, 1)
        t_ref[size - 8 :, :] = pltpu.roll(tile, size - 8, 1)
        return 0

    rounds = size // 8
    parts = len(between) + 1
    edges = [rounds * i // parts for i in range(parts + 1)]
    for i in range(parts):
        lax.fori_loop(edges[i], edges[i + 1], round_of, 0)
        if i < len(between):
            between[i]()
    t = t_ref[...]
    pivot = jnp.sum(jnp.where(row == lane, t, 0.0), axis=1, keepdims=True)
    unit = jnp.where(row > lane, t, jnp.where(row == lane, 1.0, 0.0))
    return unit * lax.rsqrt(pivot)


def kernel(
    n, nsp,
    vals, scales, slab, slab_sc, test, owner, offset,
    basis_o, coef_o,
    win, win_s, msc, place, tm_out, tm_in, part, rs_out, rs_in, sk, skt,
    gr, g_out, g_in, g_fin, cr, c_out, c_in, c_fin, sl_in, t_ref, inv_ref,
    tm_ss, tm_rs, rr_ss, rr_rs, rl_ss, rl_rs, ar_ss, ar_rs, al_ss, al_rs,
    g_ss, g_rs, c_ss, c_rs, sl_ss, sl_rs,
):
    z = lax.axis_index("slot")
    me = lax.axis_index("space")
    core = lax.rem(me, 2)
    rows, cols = vals.shape
    rank = test.shape[1]
    block = rows // scales.shape[0]
    sc = slab.shape[1]
    sw = sl_in.shape[2]
    nb = nsp.bit_length() - 1
    half = rank // 2
    chunk = rows // n
    sub = chunk // SUB
    total_rows = rows * nsp

    strides = [jnp.int32(1)]
    for i in range(1, nb):
        strides.append((1 << i) * (1 - core) + (1 << (nb - i)) * core)
    strides.append(jnp.int32(1))

    def partner(stride):
        return me + stride * (1 - 2 * lax.rem(me // stride, 2))

    def copy(src, dst, ss, rs, space=None, slot=None):
        return pltpu.make_async_remote_copy(
            src_ref=src, dst_ref=dst, send_sem=ss, recv_sem=rs,
            device_id={"space": me if space is None else space, "slot": z if slot is None else slot},
            device_id_type=MESH,
        )

    barrier = pltpu.get_barrier_semaphore()
    for d in range(1, n):
        pl.semaphore_signal(
            barrier, inc=1, device_id={"space": me, "slot": lax.rem(z + d, n)}, device_id_type=MESH
        )
    for i in range(nb):
        pl.semaphore_signal(
            barrier, inc=1, device_id={"space": partner(jnp.int32(1 << i)), "slot": z}, device_id_type=MESH
        )

    first = jnp.where(owner[0] == z, offset[0], -(2 ** 20))

    @pl.loop(0, n)
    def _(s):
        diff = lax.broadcasted_iota(jnp.int32, (sc, cols), 1) - lax.broadcasted_iota(
            jnp.int32, (sc, cols), 0
        )
        one_hot = jnp.where(diff == first + s * sc, 1.0, 0.0).astype(BF16)
        place[pl.ds(pl.multiple_of(s * sc, sc), sc), :] = one_hot
        tm_out[s] = dot(one_hot, test[...]).astype(BF16)

    pl.semaphore_wait(barrier, n - 1 + nb)

    def tm_copy(d):
        peer = lax.rem(z + d, n)
        return copy(tm_out.at[peer], tm_in.at[d], tm_ss.at[d], tm_rs.at[d], slot=peer)

    for d in range(1, n):
        tm_copy(d).start()

    col = lax.broadcasted_iota(jnp.int32, scales.shape, 1) - first
    replaced = (col >= 0) & (col < n * sc)
    msc[...] = jnp.where(replaced, 0.0, scales[...].astype(F32))

    ssc = slab_sc[...].astype(F32)
    for b in range(rows // block):
        win_s[b * block : (b + 1) * block, :] = (
            slab[b * block : (b + 1) * block, :].astype(F32) * ssc[b : b + 1, :]
        ).astype(BF16)

    @pl.loop(0, rows // block)
    def _(b):
        at = pl.ds(pl.multiple_of(b * block, block), block)
        w = (vals[at, :].astype(F32) * msc[pl.ds(b, 1), :]).astype(BF16)
        win[at, :] = w
        part[at, :] = dot(w, test[...])

    rows_new = tm_out[z].astype(F32)
    for d in range(1, n):
        tm_copy(d).wait_recv()
        rows_new += tm_in[d].astype(F32)
    rows_new = rows_new.astype(BF16)

    @pl.loop(0, n)
    def _(c):
        at = pl.ds(pl.multiple_of(c * chunk, chunk), chunk)
        part[at, :] += dot(win_s[at, :], rows_new)

    def span(c, h):
        return pl.ds(pl.multiple_of(c * chunk + h * sub, sub), sub)

    def rs_copy(way, c, h):
        ss, rs = ((rr_ss, rr_rs), (rl_ss, rl_rs))[way]
        step = 1 - 2 * way
        at = span(c, h)
        return copy(
            rs_out.at[way, at], rs_in.at[way, at], ss.at[c, h], rs.at[c, h], slot=z + step
        )

    has = (z > 0, z < n - 1)
    for d in range(n - 1, 0, -1):
        for h in range(SUB):
            for way in (0, 1):
                c = z + d * (1 - 2 * way)

                @pl.when((c >= 0) & (c < n))
                def _():
                    at = span(c, h)

                    @pl.when(has[way])
                    def _():
                        rs_copy(way, c, h).wait_recv()
                        part[at, :] += rs_in[way, at, :].astype(F32)

                    rs_out[way, at, :] = part[at, :].astype(BF16)
                    rs_copy(way, c, h).start()

    def ag_copy(way, c, h):
        ss, rs = ((ar_ss, ar_rs), (al_ss, al_rs))[way]
        at = span(c, h)
        return copy(sk.at[at], sk.at[at], ss.at[c, h], rs.at[c, h], slot=z + 1 - 2 * way)

    for h in range(SUB):
        at = span(z, h)
        for way in (0, 1):

            @pl.when(has[way])
            def _():
                rs_copy(way, z, h).wait_recv()
                part[at, :] += rs_in[way, at, :].astype(F32)

        sk[at, :] = part[at, :].astype(BF16)
        for way in (0, 1):

            @pl.when(has[1 - way])
            def _():
                ag_copy(way, z, h).start()

    for d in range(1, n):
        for h in range(SUB):
            for way in (0, 1):
                c = z - d * (1 - 2 * way)

                @pl.when((c >= 0) & (c < n))
                def _():
                    ag_copy(way, c, h).wait_recv()

                    @pl.when(has[1 - way])
                    def _():
                        ag_copy(way, c, h).start()

    @pl.loop(0, n)
    def _(c):
        at = pl.ds(pl.multiple_of(c * chunk, chunk), chunk)
        skt[:, at] = sk[at, :].astype(F32).T.astype(BF16)

    def half_at(c):
        return pl.ds(pl.multiple_of(c * half, half), half)

    def g_copy(i):
        if i == 0:
            return copy(gr.at[half_at(1 - core)], g_in.at[0], g_ss.at[0], g_rs.at[0], space=partner(strides[0]))
        if i < nb:
            return copy(g_out.at[i], g_in.at[i], g_ss.at[i], g_rs.at[i], space=partner(strides[i]))
        at = half_at(core)
        return copy(g_fin.at[at], g_fin.at[at], g_ss.at[i], g_rs.at[i], space=partner(strides[0]))

    def g_step(i):
        own = gr[half_at(core), :] if i == 1 else g_out[i - 1]
        g_copy(i - 1).wait_recv()
        total = own + g_in[i - 1]
        if i < nb:
            g_out[i] = total
        else:
            g_fin[half_at(core), :] = total
        g_copy(i).start()

    gr[...] = dot(skt[...], sk[...])
    g_copy(0).start()

    width = 2 * rank if cols % (2 * rank) == 0 else rank
    blocks = cols // width
    cr[:, cols:] = jnp.zeros((rank, sw), F32)
    cr[:, cols : cols + sc] = dot(skt[...], win_s[...])
    for i in range(nb):

        @pl.loop(blocks * i // nb, blocks * (i + 1) // nb)
        def _(b):
            at = pl.ds(pl.multiple_of(b * width, width), width)
            cr[:, at] = dot(skt[...], win[:, at])

        if i + 1 < nb:
            g_step(i + 1)

    def c_copy(i):
        if i < nb:
            return copy(c_out.at[i], c_in.at[i], c_ss.at[i], c_rs.at[i], space=partner(strides[i]))
        at = half_at(core)
        return copy(c_fin.at[at], c_fin.at[at], c_ss.at[i], c_rs.at[i], space=partner(strides[0]))

    c_out[0] = cr[half_at(1 - core), :].astype(BF16)
    c_copy(0).start()

    def c_step(i):
        c_copy(i - 1).wait_recv()
        own = cr[half_at(core), :] if i == 1 else c_out[i - 1].astype(F32)
        total = (own + c_in[i - 1].astype(F32)).astype(BF16)
        if i < nb:
            c_out[i] = total
        else:
            c_fin[half_at(core), :] = total
        c_copy(i).start()

    def sl_copy(d):
        return copy(
            c_fin.at[:, pl.ds(cols, sw)], sl_in.at[d], sl_ss.at[d], sl_rs.at[d], slot=lax.rem(z + d, n)
        )

    def sl_start():
        c_copy(nb).wait_recv()
        for d in range(1, n):
            sl_copy(d).start()

    g_step(nb)
    c_step(1)
    g_copy(nb).wait_recv()

    steps = [functools.partial(c_step, i) for i in range(2, nb + 1)] + [sl_start]
    cut = (len(steps) + 1) // 2
    scale = 1.0 / total_rows
    t_ref[...] = g_fin[:half, :half] * scale
    inv1 = inverse_lower(t_ref, half, steps[:cut])
    low = dot_full(g_fin[half:, :half] * scale, inv1, ((1,), (1,)))
    t_ref[...] = g_fin[half:, half:] * scale - dot_full(low, low, ((1,), (1,)))
    inv2 = inverse_lower(t_ref, half, steps[cut:])
    inv_ref[:half, :half] = inv1
    inv_ref[:half, half:] = jnp.zeros((half, half), F32)
    inv_ref[half:, :half] = -dot_full(inv2, dot_full(low, inv1))
    inv_ref[half:, half:] = inv2

    hi, lo = split(inv_ref[...])

    @pl.loop(0, n)
    def _(c):
        at = pl.ds(pl.multiple_of(c * chunk, chunk), chunk)
        s = sk[at, :]
        basis_o[at, :] = (dot(s, hi, ((1,), (1,))) + dot(s, lo, ((1,), (1,)))).astype(BF16)

    for d in range(1, n):
        sl_copy(d).wait_recv()
    norm = 1.0 / (total_rows ** 0.5)

    @pl.loop(0, blocks)
    def _(b):
        at = pl.ds(pl.multiple_of(b * width, width), width)
        x = c_fin[:, at].astype(F32)
        for d in range(n):
            src = lax.rem(z + n - d, n)
            p = place[pl.ds(pl.multiple_of(src * sc, sc), sc), at]
            own = c_fin[:, cols : cols + sc] if d == 0 else sl_in[d, :, :sc]
            x += dot(own, p)
        x = x.astype(BF16)
        coef_o[:, at] = (dot(hi, x) + dot(lo, x)) * norm

    for d in range(1, n):
        tm_copy(d).wait_send()
        sl_copy(d).wait_send()
        for h in range(SUB):
            for way in (0, 1):
                c = z + d * (1 - 2 * way)

                @pl.when((c >= 0) & (c < n))
                def _():
                    rs_copy(way, c, h).wait_send()

    for d in range(n):
        for h in range(SUB):
            for way in (0, 1):
                c = z - d * (1 - 2 * way)

                @pl.when((c >= 0) & (c < n) & has[1 - way])
                def _():
                    ag_copy(way, c, h).wait_send()

    for i in range(nb + 1):
        g_copy(i).wait_send()
        c_copy(i).wait_send()


def local(n, nsp, vals, scales, slab, slab_sc, test, owner, offset):
    rows, cols = vals.shape
    rank = test.shape[1]
    sc = slab.shape[1]
    sw = -(-sc // 128) * 128
    nb = nsp.bit_length() - 1
    half = rank // 2
    vmem = pl.BlockSpec(memory_space=pltpu.VMEM)
    smem = pl.BlockSpec(memory_space=pltpu.SMEM)
    dma = pltpu.SemaphoreType.DMA
    flops = 2 * rank * (2 * rows * cols + 3 * rank * rows + 2 * rank * cols)
    return pl.pallas_call(
        functools.partial(kernel, n, nsp),
        out_shape=(
            jax.ShapeDtypeStruct((rows, rank), BF16),
            jax.ShapeDtypeStruct((rank, cols), F32),
        ),
        in_specs=[vmem] * 5 + [smem] * 2,
        out_specs=(vmem, vmem),
        scratch_shapes=[
            pltpu.VMEM((rows, cols), BF16),
            pltpu.VMEM((rows, sc), BF16),
            pltpu.VMEM(scales.shape, F32),
            pltpu.VMEM((n * sc, cols), BF16),
            pltpu.VMEM((n, sc, rank), BF16),
            pltpu.VMEM((n, sc, rank), BF16),
            pltpu.VMEM((rows, rank), F32),
            pltpu.VMEM((2, rows, rank), BF16),
            pltpu.VMEM((2, rows, rank), BF16),
            pltpu.VMEM((rows, rank), BF16),
            pltpu.VMEM((rank, rows), BF16),
            pltpu.VMEM((rank, rank), F32),
            pltpu.VMEM((nb, half, rank), F32),
            pltpu.VMEM((nb, half, rank), F32),
            pltpu.VMEM((rank, rank), F32),
            pltpu.VMEM((rank, cols + sw), F32),
            pltpu.VMEM((nb, half, cols + sw), BF16),
            pltpu.VMEM((nb, half, cols + sw), BF16),
            pltpu.VMEM((rank, cols + sw), BF16),
            pltpu.VMEM((n, rank, sw), BF16),
            pltpu.VMEM((half, half), F32),
            pltpu.VMEM((rank, rank), F32),
            dma((n,)), dma((n,)),
            dma((n, SUB)), dma((n, SUB)), dma((n, SUB)), dma((n, SUB)),
            dma((n, SUB)), dma((n, SUB)), dma((n, SUB)), dma((n, SUB)),
            dma((nb + 1,)), dma((nb + 1,)), dma((nb + 1,)), dma((nb + 1,)),
            dma((n,)), dma((n,)),
        ],
        compiler_params=pltpu.CompilerParams(
            collective_id=0, has_side_effects=True, vmem_limit_bytes=60 * 2 ** 20
        ),
        cost_estimate=pl.CostEstimate(
            flops=flops, bytes_accessed=2 * rows * cols + 4 * rank * cols, transcendentals=0
        ),
    )(vals, scales, slab, slab_sc, test, owner, offset)


def solution(mesh):
    return jax.shard_map(
        functools.partial(local, mesh.shape["slot"], mesh.shape["space"]),
        mesh=mesh,
        in_specs=(
            P("space", "slot"),
            P("space", "slot"),
            P("space", "slot"),
            P("space", "slot"),
            P("slot", None),
            P(),
            P(),
        ),
        out_specs=(P("space", None), P(None, "slot")),
        check_vma=False,
    )
```

```python
import functools

import jax
import jax.numpy as jnp
from jax import lax
from jax.experimental import pallas as pl
from jax.experimental.pallas import tpu as pltpu
from jax.sharding import PartitionSpec as P

MESH = pl.DeviceIdType.MESH
F32, BF16 = jnp.float32, jnp.bfloat16
SUB = 4
PIECES = 4


def dot(a, b, contract=((1,), (0,))):
    return lax.dot_general(a, b, (contract, ((), ())), preferred_element_type=F32)


def dot_full(a, b, contract=((1,), (0,))):
    return lax.dot_general(
        a, b, (contract, ((), ())), precision=lax.Precision.HIGHEST, preferred_element_type=F32
    )


def split(x):
    hi = x.astype(BF16)
    return hi, (x - hi.astype(F32)).astype(BF16)


def inverse_lower(t_ref, size, between):
    row = lax.broadcasted_iota(jnp.int32, (size, size), 0)
    lane = lax.broadcasted_iota(jnp.int32, (size, size), 1)
    sub8 = lax.broadcasted_iota(jnp.int32, (8, size), 0)
    lane8 = lax.broadcasted_iota(jnp.int32, (8, size), 1)
    lane1 = lax.broadcasted_iota(jnp.int32, (1, size), 1)

    def round_of(g, _):
        rest = t_ref[8:, :]
        tile = t_ref[:8, :]
        cols = [jnp.broadcast_to(tile[:, j : j + 1], (8, size)) for j in range(8)]
        inv8 = jnp.zeros((8, size), F32)
        for s in range(8):
            inv = 1.0 / cols[s][s : s + 1, :]
            inv8 = jnp.where(sub8 == s, inv, inv8)
            m = jnp.where(sub8 > s, cols[s] * inv, 0.0)
            r = jnp.where(lane1 == s, 1.0, tile[s : s + 1, :])
            for j in range(s + 1, 8):
                cols[j] = cols[j] - m * cols[j][s : s + 1, :]
            tile = jnp.where((sub8 > s) & (lane8 == s), 0.0, tile) - m * r
        left = size - 8 * g
        mult = jnp.where((lane8 >= 8) & (lane8 < left), tile * inv8, 0.0)
        unit = jnp.where(lane8 < sub8, tile, jnp.where(lane8 == sub8, 1.0, 0.0))
        rows = jnp.where(lane8 < 8, unit, tile)
        change = dot_full(mult, rows, ((0,), (0,)))
        open_rows = (row[8:] < left) & (lane[8:] < 8)
        rest = jnp.where(open_rows, 0.0, rest) - change[8:]
        t_ref[: size - 8, :] = pltpu.roll(rest, size - 8, 1)
        t_ref[size - 8 :, :] = pltpu.roll(tile, size - 8, 1)
        return 0

    done, rounds = 0, size // 8
    for at, action in between:
        at = min(int(at * rounds), rounds)
        lax.fori_loop(done, at, round_of, 0)
        action()
        done = at
    lax.fori_loop(done, rounds, round_of, 0)
    t = t_ref[...]
    pivot = jnp.sum(jnp.where(row == lane, t, 0.0), axis=1, keepdims=True)
    unit = jnp.where(row > lane, t, jnp.where(row == lane, 1.0, 0.0))
    return unit * lax.rsqrt(pivot)


def kernel(
    n, nsp,
    vals, scales, slab, slab_sc, test, owner, offset,
    sk_o, x_o, inv_ref,
    vbuf, win, win_s, msc, place, tm_out, tm_in, part, rs_out, rs_in, sk, skt,
    gr, g_out, g_in, g_fin, cr, c_out, c_in, c_fin, sl_in, t_ref, gpart,
    tm_ss, tm_rs, rr_ss, rr_rs, rl_ss, rl_rs, ar_ss, ar_rs, al_ss, al_rs,
    g_ss, g_rs, c_ss, c_rs, sl_ss, sl_rs, v_sem, o_sem,
):
    z = lax.axis_index("slot")
    me = lax.axis_index("space")
    core = lax.rem(me, 2)
    rows, cols = vals.shape
    rank = test.shape[1]
    block = rows // scales.shape[0]
    sc = slab.shape[1]
    sw = sl_in.shape[2]
    nb = nsp.bit_length() - 1
    half = rank // 2
    chunk = rows // n
    sub = chunk // SUB
    total_rows = rows * nsp

    strides = [jnp.int32(1)]
    for i in range(1, nb):
        strides.append((1 << i) * (1 - core) + (1 << (nb - i)) * core)
    strides.append(jnp.int32(1))

    def partner(stride):
        return me + stride * (1 - 2 * lax.rem(me // stride, 2))

    def copy(src, dst, ss, rs, space=None, slot=None):
        return pltpu.make_async_remote_copy(
            src_ref=src, dst_ref=dst, send_sem=ss, recv_sem=rs,
            device_id={"space": me if space is None else space, "slot": z if slot is None else slot},
            device_id_type=MESH,
        )

    def load(c):
        at = pl.ds(pl.multiple_of(c * chunk, chunk), chunk)
        return pltpu.make_async_copy(vals.at[at], vbuf.at[at], v_sem.at[c])

    for c in range(n):
        load(c).start()

    barrier = pltpu.get_barrier_semaphore()
    for d in range(1, n):
        pl.semaphore_signal(
            barrier, inc=1, device_id={"space": me, "slot": lax.rem(z + d, n)}, device_id_type=MESH
        )
    for i in range(nb):
        pl.semaphore_signal(
            barrier, inc=1, device_id={"space": partner(jnp.int32(1 << i)), "slot": z}, device_id_type=MESH
        )

    first = jnp.where(owner[0] == z, offset[0], -(2 ** 20))

    @pl.loop(0, n)
    def _(s):
        diff = lax.broadcasted_iota(jnp.int32, (sc, cols), 1) - lax.broadcasted_iota(
            jnp.int32, (sc, cols), 0
        )
        one_hot = jnp.where(diff == first + s * sc, 1.0, 0.0).astype(BF16)
        place[pl.ds(pl.multiple_of(s * sc, sc), sc), :] = one_hot
        tm_out[s] = dot(one_hot, test[...]).astype(BF16)

    pl.semaphore_wait(barrier, n - 1 + nb)

    def tm_copy(d):
        peer = lax.rem(z + d, n)
        return copy(tm_out.at[peer], tm_in.at[d], tm_ss.at[d], tm_rs.at[d], slot=peer)

    for d in range(1, n):
        tm_copy(d).start()

    col = lax.broadcasted_iota(jnp.int32, scales.shape, 1) - first
    replaced = (col >= 0) & (col < n * sc)
    msc[...] = jnp.where(replaced, 0.0, scales[...].astype(F32))

    ssc = slab_sc[...].astype(F32)
    for b in range(rows // block):
        win_s[b * block : (b + 1) * block, :] = (
            slab[b * block : (b + 1) * block, :].astype(F32) * ssc[b : b + 1, :]
        ).astype(BF16)

    @pl.loop(0, n)
    def _(c):
        load(c).wait()

        @pl.loop(0, chunk // block)
        def _(i):
            b = c * (chunk // block) + i
            at = pl.ds(pl.multiple_of(b * block, block), block)
            w = (vbuf[at, :].astype(F32) * msc[pl.ds(b, 1), :]).astype(BF16)
            win[at, :] = w
            part[at, :] = dot(w, test[...])

    rows_new = tm_out[z].astype(F32)
    for d in range(1, n):
        tm_copy(d).wait_recv()
        rows_new += tm_in[d].astype(F32)
    rows_new = rows_new.astype(BF16)

    def add_new(c):
        at = pl.ds(pl.multiple_of(c * chunk, chunk), chunk)
        part[at, :] += dot(win_s[at, :], rows_new)

    def span(c, h):
        return pl.ds(pl.multiple_of(c * chunk + h * sub, sub), sub)

    def rs_copy(way, c, h):
        ss, rs = ((rr_ss, rr_rs), (rl_ss, rl_rs))[way]
        step = 1 - 2 * way
        at = span(c, h)
        return copy(
            rs_out.at[way, at], rs_in.at[way, at], ss.at[c, h], rs.at[c, h], slot=z + step
        )

    has = (z > 0, z < n - 1)
    for d in range(n - 1, 0, -1):
        for way in (0, 1):
            c = z + d * (1 - 2 * way)

            @pl.when((c >= 0) & (c < n))
            def _():
                add_new(c)

        for h in range(SUB):
            for way in (0, 1):
                c = z + d * (1 - 2 * way)

                @pl.when((c >= 0) & (c < n))
                def _():
                    at = span(c, h)

                    @pl.when(has[way])
                    def _():
                        rs_copy(way, c, h).wait_recv()
                        part[at, :] += rs_in[way, at, :].astype(F32)

                    rs_out[way, at, :] = part[at, :].astype(BF16)
                    rs_copy(way, c, h).start()

    add_new(z)

    def ag_copy(way, c, h):
        ss, rs = ((ar_ss, ar_rs), (al_ss, al_rs))[way]
        at = span(c, h)
        return copy(sk.at[at], sk.at[at], ss.at[c, h], rs.at[c, h], slot=z + 1 - 2 * way)

    for h in range(SUB):
        at = span(z, h)
        for way in (0, 1):

            @pl.when(has[way])
            def _():
                rs_copy(way, z, h).wait_recv()
                part[at, :] += rs_in[way, at, :].astype(F32)

        sk[at, :] = part[at, :].astype(BF16)
        for way in (0, 1):

            @pl.when(has[1 - way])
            def _():
                ag_copy(way, z, h).start()

    width = 2 * rank if cols % (2 * rank) == 0 else rank
    blocks = cols // width
    cr[...] = jnp.zeros(cr.shape, F32)

    def gram_of(c):
        at = pl.ds(pl.multiple_of(c * chunk, chunk), chunk)
        s = sk[at, :]
        t = s.astype(F32).T.astype(BF16)
        skt[:, at] = t
        gpart[c] = dot(t, s)

    def cross_of(c):
        at = pl.ds(pl.multiple_of(c * chunk, chunk), chunk)
        t = skt[:, at]
        cr[:, cols : cols + sc] += dot(t, win_s[at, :])

        @pl.loop(0, blocks)
        def _(b):
            to = pl.ds(pl.multiple_of(b * width, width), width)
            cr[:, to] += dot(t, win[at, to])

    def at_distance(d, action):
        for c in (z - d, z + d)[: 2 if d else 1]:

            @pl.when((c >= 0) & (c < n))
            def _():
                action(c)

    gram_of(z)
    for d in range(1, n):
        at_distance(d - 1, cross_of)
        for h in range(SUB):
            for way in (0, 1):
                c = z - d * (1 - 2 * way)

                @pl.when((c >= 0) & (c < n))
                def _():
                    ag_copy(way, c, h).wait_recv()

                    @pl.when(has[1 - way])
                    def _():
                        ag_copy(way, c, h).start()

        at_distance(d, gram_of)

    out_sk = pltpu.make_async_copy(sk, sk_o, o_sem.at[0])
    out_sk.start()

    def half_at(c):
        return pl.ds(pl.multiple_of(c * half, half), half)

    def g_copy(i):
        if i == 0:
            return copy(gr.at[half_at(1 - core)], g_in.at[0], g_ss.at[0], g_rs.at[0], space=partner(strides[0]))
        if i < nb:
            return copy(g_out.at[i], g_in.at[i], g_ss.at[i], g_rs.at[i], space=partner(strides[i]))
        at = half_at(core)
        return copy(g_fin.at[at], g_fin.at[at], g_ss.at[i], g_rs.at[i], space=partner(strides[0]))

    def g_step(i):
        own = gr[half_at(core), :] if i == 1 else g_out[i - 1]
        g_copy(i - 1).wait_recv()
        total = own + g_in[i - 1]
        if i < nb:
            g_out[i] = total
        else:
            g_fin[half_at(core), :] = total
        g_copy(i).start()

    total = gpart[0]
    for c in range(1, n):
        total += gpart[c]
    gr[...] = total
    g_copy(0).start()
    at_distance(n - 1, cross_of)
    for i in range(1, nb):
        g_step(i)

    def c_copy(i):
        if i < nb:
            return copy(c_out.at[i], c_in.at[i], c_ss.at[i], c_rs.at[i], space=partner(strides[i]))
        at = half_at(core)
        return copy(c_fin.at[at], c_fin.at[at], c_ss.at[i], c_rs.at[i], space=partner(strides[0]))

    c_out[0] = cr[half_at(1 - core), :].astype(BF16)
    c_copy(0).start()

    def c_step(i):
        c_copy(i - 1).wait_recv()
        own = cr[half_at(core), :] if i == 1 else c_out[i - 1].astype(F32)
        total = (own + c_in[i - 1].astype(F32)).astype(BF16)
        if i < nb:
            c_out[i] = total
        else:
            c_fin[half_at(core), :] = total
        c_copy(i).start()

    def sl_copy(d):
        return copy(
            c_fin.at[:, pl.ds(cols, sw)], sl_in.at[d], sl_ss.at[d], sl_rs.at[d], slot=lax.rem(z + d, n)
        )

    def sl_start():
        c_copy(nb).wait_recv()
        for d in range(1, n):
            sl_copy(d).start()

    g_step(nb)
    c_step(1)
    g_copy(nb).wait_recv()

    steps = [functools.partial(c_step, i) for i in range(2, nb + 1)] + [sl_start]
    spots = [(0.5 + i * 1.0 / len(steps), f) for i, f in enumerate(steps)]
    early = [(at, f) for at, f in spots if at < 1]
    late = [(at - 1, f) for at, f in spots if at >= 1]
    scale = 1.0 / total_rows
    t_ref[...] = g_fin[:half, :half] * scale
    inv1 = inverse_lower(t_ref, half, early)
    low = dot_full(g_fin[half:, :half] * scale, inv1, ((1,), (1,)))
    t_ref[...] = g_fin[half:, half:] * scale - dot_full(low, low, ((1,), (1,)))
    inv2 = inverse_lower(t_ref, half, late)
    inv_ref[:half, :half] = inv1
    inv_ref[:half, half:] = jnp.zeros((half, half), F32)
    inv_ref[half:, :half] = -dot_full(inv2, dot_full(low, inv1))
    inv_ref[half:, half:] = inv2

    for d in range(1, n):
        sl_copy(d).wait_recv()

    @pl.loop(0, blocks)
    def _(b):
        at = pl.ds(pl.multiple_of(b * width, width), width)
        x = c_fin[:, at].astype(F32)
        for d in range(n):
            src = lax.rem(z + n - d, n)
            p = place[pl.ds(pl.multiple_of(src * sc, sc), sc), at]
            own = c_fin[:, cols : cols + sc] if d == 0 else sl_in[d, :, :sc]
            x += dot(own, p)
        x_o[:, at] = x.astype(BF16)

    for d in range(1, n):
        tm_copy(d).wait_send()
        sl_copy(d).wait_send()
        for h in range(SUB):
            for way in (0, 1):
                c = z + d * (1 - 2 * way)

                @pl.when((c >= 0) & (c < n))
                def _():
                    rs_copy(way, c, h).wait_send()

    for d in range(n):
        for h in range(SUB):
            for way in (0, 1):
                c = z - d * (1 - 2 * way)

                @pl.when((c >= 0) & (c < n) & has[1 - way])
                def _():
                    ag_copy(way, c, h).wait_send()

    for i in range(nb + 1):
        g_copy(i).wait_send()
        c_copy(i).wait_send()
    out_sk.wait()


def apply(total_rows, sk, x, inv, basis_o, coef_o):
    hi, lo = split(inv[...])
    s = sk[...]
    basis_o[...] = (dot(s, hi, ((1,), (1,))) + dot(s, lo, ((1,), (1,)))).astype(BF16)
    v = x[...]
    coef_o[...] = (dot(hi, v) + dot(lo, v)) * (1.0 / total_rows ** 0.5)


def local(n, nsp, vals, scales, slab, slab_sc, test, owner, offset):
    rows, cols = vals.shape
    rank = test.shape[1]
    sc = slab.shape[1]
    sw = -(-sc // 128) * 128
    nb = nsp.bit_length() - 1
    half = rank // 2
    vmem = pl.BlockSpec(memory_space=pltpu.VMEM)
    smem = pl.BlockSpec(memory_space=pltpu.SMEM)
    dma = pltpu.SemaphoreType.DMA
    flops = 2 * rank * (2 * rows * cols + 3 * rank * rows + 2 * rank * cols)
    sk, x, inv = pl.pallas_call(
        functools.partial(kernel, n, nsp),
        out_shape=(
            jax.ShapeDtypeStruct((rows, rank), BF16),
            jax.ShapeDtypeStruct((rank, cols), BF16),
            jax.ShapeDtypeStruct((rank, rank), F32),
        ),
        in_specs=[pl.BlockSpec(memory_space=pl.ANY)] + [vmem] * 4 + [smem] * 2,
        out_specs=(pl.BlockSpec(memory_space=pl.ANY), vmem, vmem),
        scratch_shapes=[
            pltpu.VMEM((rows, cols), BF16),
            pltpu.VMEM((rows, cols), BF16),
            pltpu.VMEM((rows, sc), BF16),
            pltpu.VMEM(scales.shape, F32),
            pltpu.VMEM((n * sc, cols), BF16),
            pltpu.VMEM((n, sc, rank), BF16),
            pltpu.VMEM((n, sc, rank), BF16),
            pltpu.VMEM((rows, rank), F32),
            pltpu.VMEM((2, rows, rank), BF16),
            pltpu.VMEM((2, rows, rank), BF16),
            pltpu.VMEM((rows, rank), BF16),
            pltpu.VMEM((rank, rows), BF16),
            pltpu.VMEM((rank, rank), F32),
            pltpu.VMEM((nb, half, rank), F32),
            pltpu.VMEM((nb, half, rank), F32),
            pltpu.VMEM((rank, rank), F32),
            pltpu.VMEM((rank, cols + sw), F32),
            pltpu.VMEM((nb, half, cols + sw), BF16),
            pltpu.VMEM((nb, half, cols + sw), BF16),
            pltpu.VMEM((rank, cols + sw), BF16),
            pltpu.VMEM((n, rank, sw), BF16),
            pltpu.VMEM((half, half), F32),
            pltpu.VMEM((n, rank, rank), F32),
            dma((n,)), dma((n,)),
            dma((n, SUB)), dma((n, SUB)), dma((n, SUB)), dma((n, SUB)),
            dma((n, SUB)), dma((n, SUB)), dma((n, SUB)), dma((n, SUB)),
            dma((nb + 1,)), dma((nb + 1,)), dma((nb + 1,)), dma((nb + 1,)),
            dma((n,)), dma((n,)), dma((n,)), dma((1,)),
        ],
        compiler_params=pltpu.CompilerParams(
            collective_id=0, has_side_effects=True, vmem_limit_bytes=60 * 2 ** 20
        ),
        cost_estimate=pl.CostEstimate(
            flops=flops, bytes_accessed=2 * rows * cols + 4 * rank * cols, transcendentals=0
        ),
    )(vals, scales, slab, slab_sc, test, owner, offset)
    return pl.pallas_call(
        functools.partial(apply, rows * nsp),
        out_shape=(
            jax.ShapeDtypeStruct((rows, rank), BF16),
            jax.ShapeDtypeStruct((rank, cols), F32),
        ),
        grid=(PIECES,),
        in_specs=[
            pl.BlockSpec((rows // PIECES, rank), lambda i: (i, 0)),
            pl.BlockSpec((rank, cols // PIECES), lambda i: (0, i)),
            pl.BlockSpec((rank, rank), lambda i: (0, 0)),
        ],
        out_specs=(
            pl.BlockSpec((rows // PIECES, rank), lambda i: (i, 0)),
            pl.BlockSpec((rank, cols // PIECES), lambda i: (0, i)),
        ),
        cost_estimate=pl.CostEstimate(
            flops=4 * rank * rank * (rows + cols), bytes_accessed=4 * rank * (rows + cols),
            transcendentals=0,
        ),
    )(sk, x, inv)


def solution(mesh):
    return jax.shard_map(
        functools.partial(local, mesh.shape["slot"], mesh.shape["space"]),
        mesh=mesh,
        in_specs=(
            P("space", "slot"),
            P("space", "slot"),
            P("space", "slot"),
            P("space", "slot"),
            P("slot", None),
            P(),
            P(),
        ),
        out_specs=(P("space", None), P(None, "slot")),
        check_vma=False,
    )
```

```python
import functools

import jax
import jax.numpy as jnp
from jax import lax
from jax.experimental import pallas as pl
from jax.experimental.pallas import tpu as pltpu
from jax.sharding import PartitionSpec as P

MESH = pl.DeviceIdType.MESH
F32, BF16 = jnp.float32, jnp.bfloat16
SUB = 4
PIECES = 4
WIDE = 16


def dot(a, b, contract=((1,), (0,))):
    return lax.dot_general(a, b, (contract, ((), ())), preferred_element_type=F32)


def dot_full(a, b, contract=((1,), (0,))):
    return lax.dot_general(
        a, b, (contract, ((), ())), precision=lax.Precision.HIGHEST, preferred_element_type=F32
    )


def split(x):
    hi = x.astype(BF16)
    return hi, (x - hi.astype(F32)).astype(BF16)


def inverse_lower(t_ref, size, between):
    row = lax.broadcasted_iota(jnp.int32, (size, size), 0)
    lane = lax.broadcasted_iota(jnp.int32, (size, size), 1)
    sub = lax.broadcasted_iota(jnp.int32, (WIDE, size), 0)
    lane_t = lax.broadcasted_iota(jnp.int32, (WIDE, size), 1)
    lane1 = lax.broadcasted_iota(jnp.int32, (1, size), 1)

    def round_of(g, _):
        rest = t_ref[WIDE:, :]
        tile = t_ref[:WIDE, :]
        cols = [jnp.broadcast_to(tile[:, j : j + 1], (WIDE, size)) for j in range(WIDE)]
        inv_t = jnp.zeros((WIDE, size), F32)
        for s in range(WIDE):
            inv = 1.0 / cols[s][s : s + 1, :]
            inv_t = jnp.where(sub == s, inv, inv_t)
            m = jnp.where(sub > s, cols[s], 0.0) * inv
            r = jnp.where(lane1 == s, 1.0, tile[s : s + 1, :])
            for j in range(s + 1, WIDE):
                cols[j] = cols[j] - m * cols[j][s : s + 1, :]
            tile = jnp.where((sub > s) & (lane_t == s), 0.0, tile) - m * r
        left = size - WIDE * g
        mult = jnp.where((lane_t >= WIDE) & (lane_t < left), tile * inv_t, 0.0)
        unit = jnp.where(lane_t < sub, tile, jnp.where(lane_t == sub, 1.0, 0.0))
        rows = jnp.where(lane_t < WIDE, unit, tile)
        change = dot_full(mult, rows, ((0,), (0,)))
        open_rows = (row[WIDE:] < left) & (lane[WIDE:] < WIDE)
        rest = jnp.where(open_rows, 0.0, rest) - change[WIDE:]
        t_ref[: size - WIDE, :] = pltpu.roll(rest, size - WIDE, 1)
        t_ref[size - WIDE :, :] = pltpu.roll(tile, size - WIDE, 1)
        return 0

    done, rounds = 0, size // WIDE
    for at, action in between:
        at = min(int(at * rounds), rounds)
        lax.fori_loop(done, at, round_of, 0)
        action()
        done = at
    lax.fori_loop(done, rounds, round_of, 0)
    t = t_ref[...]
    pivot = jnp.sum(jnp.where(row == lane, t, 0.0), axis=1, keepdims=True)
    unit = jnp.where(row > lane, t, jnp.where(row == lane, 1.0, 0.0))
    return unit * lax.rsqrt(pivot)


def kernel(
    n, nsp,
    vals, scales, slab, slab_sc, test, owner, offset,
    sk_o, x_o, inv_ref,
    vbuf, win, win_s, msc, place, tm_out, tm_in, part, rs_out, rs_in, sk, skt,
    gr, g_out, g_in, g_fin, cr, c_out, c_in, c_fin, sl_in, t_ref, gpart,
    tm_ss, tm_rs, rr_ss, rr_rs, rl_ss, rl_rs, ar_ss, ar_rs, al_ss, al_rs,
    g_ss, g_rs, c_ss, c_rs, sl_ss, sl_rs, v_sem, o_sem,
):
    z = lax.axis_index("slot")
    me = lax.axis_index("space")
    core = lax.rem(me, 2)
    rows, cols = vals.shape
    rank = test.shape[1]
    block = rows // scales.shape[0]
    sc = slab.shape[1]
    sw = sl_in.shape[2]
    nb = nsp.bit_length() - 1
    half = rank // 2
    chunk = rows // n
    sub = chunk // SUB
    total_rows = rows * nsp

    strides = [jnp.int32(1)]
    for i in range(1, nb):
        strides.append((1 << i) * (1 - core) + (1 << (nb - i)) * core)
    strides.append(jnp.int32(1))

    def partner(stride):
        return me + stride * (1 - 2 * lax.rem(me // stride, 2))

    def copy(src, dst, ss, rs, space=None, slot=None):
        return pltpu.make_async_remote_copy(
            src_ref=src, dst_ref=dst, send_sem=ss, recv_sem=rs,
            device_id={"space": me if space is None else space, "slot": z if slot is None else slot},
            device_id_type=MESH,
        )

    def load(c):
        at = pl.ds(pl.multiple_of(c * chunk, chunk), chunk)
        return pltpu.make_async_copy(vals.at[at], vbuf.at[at], v_sem.at[c])

    for c in range(n):
        load(c).start()

    barrier = pltpu.get_barrier_semaphore()
    for d in range(1, n):
        pl.semaphore_signal(
            barrier, inc=1, device_id={"space": me, "slot": lax.rem(z + d, n)}, device_id_type=MESH
        )
    for i in range(nb):
        pl.semaphore_signal(
            barrier, inc=1, device_id={"space": partner(jnp.int32(1 << i)), "slot": z}, device_id_type=MESH
        )

    first = jnp.where(owner[0] == z, offset[0], -(2 ** 20))

    @pl.loop(0, n)
    def _(s):
        diff = lax.broadcasted_iota(jnp.int32, (sc, cols), 1) - lax.broadcasted_iota(
            jnp.int32, (sc, cols), 0
        )
        one_hot = jnp.where(diff == first + s * sc, 1.0, 0.0).astype(BF16)
        place[pl.ds(pl.multiple_of(s * sc, sc), sc), :] = one_hot
        tm_out[s] = dot(one_hot, test[...]).astype(BF16)

    pl.semaphore_wait(barrier, n - 1 + nb)

    def tm_copy(d):
        peer = lax.rem(z + d, n)
        return copy(tm_out.at[peer], tm_in.at[d], tm_ss.at[d], tm_rs.at[d], slot=peer)

    for d in range(1, n):
        tm_copy(d).start()

    col = lax.broadcasted_iota(jnp.int32, scales.shape, 1) - first
    replaced = (col >= 0) & (col < n * sc)
    msc[...] = jnp.where(replaced, 0.0, scales[...].astype(F32))

    ssc = slab_sc[...].astype(F32)
    for b in range(rows // block):
        win_s[b * block : (b + 1) * block, :] = (
            slab[b * block : (b + 1) * block, :].astype(F32) * ssc[b : b + 1, :]
        ).astype(BF16)

    @pl.loop(0, n)
    def _(c):
        load(c).wait()

        @pl.loop(0, chunk // block)
        def _(i):
            b = c * (chunk // block) + i
            at = pl.ds(pl.multiple_of(b * block, block), block)
            w = (vbuf[at, :].astype(F32) * msc[pl.ds(b, 1), :]).astype(BF16)
            win[at, :] = w
            part[at, :] = dot(w, test[...])

    rows_new = tm_out[z].astype(F32)
    for d in range(1, n):
        tm_copy(d).wait_recv()
        rows_new += tm_in[d].astype(F32)
    rows_new = rows_new.astype(BF16)

    def add_new(c):
        at = pl.ds(pl.multiple_of(c * chunk, chunk), chunk)
        part[at, :] += dot(win_s[at, :], rows_new)

    def span(c, h):
        return pl.ds(pl.multiple_of(c * chunk + h * sub, sub), sub)

    def rs_copy(way, c, h):
        ss, rs = ((rr_ss, rr_rs), (rl_ss, rl_rs))[way]
        step = 1 - 2 * way
        at = span(c, h)
        return copy(
            rs_out.at[way, at], rs_in.at[way, at], ss.at[c, h], rs.at[c, h], slot=z + step
        )

    has = (z > 0, z < n - 1)
    for d in range(n - 1, 0, -1):
        for way in (0, 1):
            c = z + d * (1 - 2 * way)

            @pl.when((c >= 0) & (c < n))
            def _():
                add_new(c)

        for h in range(SUB):
            for way in (0, 1):
                c = z + d * (1 - 2 * way)

                @pl.when((c >= 0) & (c < n))
                def _():
                    at = span(c, h)

                    @pl.when(has[way])
                    def _():
                        rs_copy(way, c, h).wait_recv()
                        part[at, :] += rs_in[way, at, :].astype(F32)

                    rs_out[way, at, :] = part[at, :].astype(BF16)
                    rs_copy(way, c, h).start()

    add_new(z)

    def ag_copy(way, c, h):
        ss, rs = ((ar_ss, ar_rs), (al_ss, al_rs))[way]
        at = span(c, h)
        return copy(sk.at[at], sk.at[at], ss.at[c, h], rs.at[c, h], slot=z + 1 - 2 * way)

    for h in range(SUB):
        at = span(z, h)
        for way in (0, 1):

            @pl.when(has[way])
            def _():
                rs_copy(way, z, h).wait_recv()
                part[at, :] += rs_in[way, at, :].astype(F32)

        sk[at, :] = part[at, :].astype(BF16)
        for way in (0, 1):

            @pl.when(has[1 - way])
            def _():
                ag_copy(way, z, h).start()

    width = 2 * rank if cols % (2 * rank) == 0 else rank
    blocks = cols // width
    cr[...] = jnp.zeros(cr.shape, F32)

    def gram_of(c):
        at = pl.ds(pl.multiple_of(c * chunk, chunk), chunk)
        s = sk[at, :]
        t = s.astype(F32).T.astype(BF16)
        skt[:, at] = t
        gpart[c] = dot(t, s)

    def cross_of(c):
        at = pl.ds(pl.multiple_of(c * chunk, chunk), chunk)
        t = skt[:, at]
        cr[:, cols : cols + sc] += dot(t, win_s[at, :])

        @pl.loop(0, blocks)
        def _(b):
            to = pl.ds(pl.multiple_of(b * width, width), width)
            cr[:, to] += dot(t, win[at, to])

    def at_distance(d, action):
        for c in (z - d, z + d)[: 2 if d else 1]:

            @pl.when((c >= 0) & (c < n))
            def _():
                action(c)

    gram_of(z)
    for d in range(1, n):
        at_distance(d - 1, cross_of)
        for h in range(SUB):
            for way in (0, 1):
                c = z - d * (1 - 2 * way)

                @pl.when((c >= 0) & (c < n))
                def _():
                    ag_copy(way, c, h).wait_recv()

                    @pl.when(has[1 - way])
                    def _():
                        ag_copy(way, c, h).start()

        at_distance(d, gram_of)

    out_sk = pltpu.make_async_copy(sk, sk_o, o_sem.at[0])
    out_sk.start()

    def half_at(c):
        return pl.ds(pl.multiple_of(c * half, half), half)

    def g_copy(i):
        if i == 0:
            return copy(gr.at[half_at(1 - core)], g_in.at[0], g_ss.at[0], g_rs.at[0], space=partner(strides[0]))
        if i < nb:
            return copy(g_out.at[i], g_in.at[i], g_ss.at[i], g_rs.at[i], space=partner(strides[i]))
        at = half_at(core)
        return copy(g_fin.at[at], g_fin.at[at], g_ss.at[i], g_rs.at[i], space=partner(strides[0]))

    def g_step(i):
        own = gr[half_at(core), :] if i == 1 else g_out[i - 1]
        g_copy(i - 1).wait_recv()
        total = own + g_in[i - 1]
        if i < nb:
            g_out[i] = total
        else:
            g_fin[half_at(core), :] = total
        g_copy(i).start()

    total = gpart[0]
    for c in range(1, n):
        total += gpart[c]
    gr[...] = total
    g_copy(0).start()
    at_distance(n - 1, cross_of)

    def c_copy(i):
        if i < nb:
            return copy(c_out.at[i], c_in.at[i], c_ss.at[i], c_rs.at[i], space=partner(strides[i]))
        at = half_at(core)
        return copy(c_fin.at[at], c_fin.at[at], c_ss.at[i], c_rs.at[i], space=partner(strides[0]))

    g_step(1)
    c_out[0] = cr[half_at(1 - core), :].astype(BF16)
    c_copy(0).start()
    for i in range(2, nb):
        g_step(i)

    def c_step(i):
        c_copy(i - 1).wait_recv()
        own = cr[half_at(core), :] if i == 1 else c_out[i - 1].astype(F32)
        total = (own + c_in[i - 1].astype(F32)).astype(BF16)
        if i < nb:
            c_out[i] = total
        else:
            c_fin[half_at(core), :] = total
        c_copy(i).start()

    def sl_copy(d):
        return copy(
            c_fin.at[:, pl.ds(cols, sw)], sl_in.at[d], sl_ss.at[d], sl_rs.at[d], slot=lax.rem(z + d, n)
        )

    def sl_start():
        c_copy(nb).wait_recv()
        for d in range(1, n):
            sl_copy(d).start()

    c_step(1)
    g_step(nb)
    g_copy(nb).wait_recv()

    steps = [functools.partial(c_step, i) for i in range(2, nb + 1)] + [sl_start]
    spots = [(0.5 + i * 1.0 / len(steps), f) for i, f in enumerate(steps)]
    early = [(at, f) for at, f in spots if at < 1]
    late = [(at - 1, f) for at, f in spots if at >= 1]
    scale = 1.0 / total_rows
    t_ref[...] = g_fin[:half, :half] * scale
    inv1 = inverse_lower(t_ref, half, early)
    low = dot_full(g_fin[half:, :half] * scale, inv1, ((1,), (1,)))
    t_ref[...] = g_fin[half:, half:] * scale - dot_full(low, low, ((1,), (1,)))
    inv2 = inverse_lower(t_ref, half, late)
    inv_ref[:half, :half] = inv1
    inv_ref[:half, half:] = jnp.zeros((half, half), F32)
    inv_ref[half:, :half] = -dot_full(inv2, dot_full(low, inv1))
    inv_ref[half:, half:] = inv2

    for d in range(1, n):
        sl_copy(d).wait_recv()

    @pl.loop(0, blocks)
    def _(b):
        at = pl.ds(pl.multiple_of(b * width, width), width)
        x = c_fin[:, at].astype(F32)
        for d in range(n):
            src = lax.rem(z + n - d, n)
            p = place[pl.ds(pl.multiple_of(src * sc, sc), sc), at]
            own = c_fin[:, cols : cols + sc] if d == 0 else sl_in[d, :, :sc]
            x += dot(own, p)
        x_o[:, at] = x.astype(BF16)

    for d in range(1, n):
        tm_copy(d).wait_send()
        sl_copy(d).wait_send()
        for h in range(SUB):
            for way in (0, 1):
                c = z + d * (1 - 2 * way)

                @pl.when((c >= 0) & (c < n))
                def _():
                    rs_copy(way, c, h).wait_send()

    for d in range(n):
        for h in range(SUB):
            for way in (0, 1):
                c = z - d * (1 - 2 * way)

                @pl.when((c >= 0) & (c < n) & has[1 - way])
                def _():
                    ag_copy(way, c, h).wait_send()

    for i in range(nb + 1):
        g_copy(i).wait_send()
        c_copy(i).wait_send()
    out_sk.wait()


def apply(total_rows, sk, x, inv, basis_o, coef_o):
    hi, lo = split(inv[...])
    s = sk[...]
    basis_o[...] = (dot(s, hi, ((1,), (1,))) + dot(s, lo, ((1,), (1,)))).astype(BF16)
    v = x[...]
    coef_o[...] = (dot(hi, v) + dot(lo, v)) * (1.0 / total_rows ** 0.5)


def local(n, nsp, vals, scales, slab, slab_sc, test, owner, offset):
    rows, cols = vals.shape
    rank = test.shape[1]
    sc = slab.shape[1]
    sw = -(-sc // 128) * 128
    nb = nsp.bit_length() - 1
    half = rank // 2
    vmem = pl.BlockSpec(memory_space=pltpu.VMEM)
    smem = pl.BlockSpec(memory_space=pltpu.SMEM)
    dma = pltpu.SemaphoreType.DMA
    flops = 2 * rank * (2 * rows * cols + 3 * rank * rows + 2 * rank * cols)
    sk, x, inv = pl.pallas_call(
        functools.partial(kernel, n, nsp),
        out_shape=(
            jax.ShapeDtypeStruct((rows, rank), BF16),
            jax.ShapeDtypeStruct((rank, cols), BF16),
            jax.ShapeDtypeStruct((rank, rank), F32),
        ),
        in_specs=[pl.BlockSpec(memory_space=pl.ANY)] + [vmem] * 4 + [smem] * 2,
        out_specs=(pl.BlockSpec(memory_space=pl.ANY), vmem, vmem),
        scratch_shapes=[
            pltpu.VMEM((rows, cols), BF16),
            pltpu.VMEM((rows, cols), BF16),
            pltpu.VMEM((rows, sc), BF16),
            pltpu.VMEM(scales.shape, F32),
            pltpu.VMEM((n * sc, cols), BF16),
            pltpu.VMEM((n, sc, rank), BF16),
            pltpu.VMEM((n, sc, rank), BF16),
            pltpu.VMEM((rows, rank), F32),
            pltpu.VMEM((2, rows, rank), BF16),
            pltpu.VMEM((2, rows, rank), BF16),
            pltpu.VMEM((rows, rank), BF16),
            pltpu.VMEM((rank, rows), BF16),
            pltpu.VMEM((rank, rank), F32),
            pltpu.VMEM((nb, half, rank), F32),
            pltpu.VMEM((nb, half, rank), F32),
            pltpu.VMEM((rank, rank), F32),
            pltpu.VMEM((rank, cols + sw), F32),
            pltpu.VMEM((nb, half, cols + sw), BF16),
            pltpu.VMEM((nb, half, cols + sw), BF16),
            pltpu.VMEM((rank, cols + sw), BF16),
            pltpu.VMEM((n, rank, sw), BF16),
            pltpu.VMEM((half, half), F32),
            pltpu.VMEM((n, rank, rank), F32),
            dma((n,)), dma((n,)),
            dma((n, SUB)), dma((n, SUB)), dma((n, SUB)), dma((n, SUB)),
            dma((n, SUB)), dma((n, SUB)), dma((n, SUB)), dma((n, SUB)),
            dma((nb + 1,)), dma((nb + 1,)), dma((nb + 1,)), dma((nb + 1,)),
            dma((n,)), dma((n,)), dma((n,)), dma((1,)),
        ],
        compiler_params=pltpu.CompilerParams(
            collective_id=0, has_side_effects=True, vmem_limit_bytes=60 * 2 ** 20
        ),
        cost_estimate=pl.CostEstimate(
            flops=flops, bytes_accessed=2 * rows * cols + 4 * rank * cols, transcendentals=0
        ),
    )(vals, scales, slab, slab_sc, test, owner, offset)
    return pl.pallas_call(
        functools.partial(apply, rows * nsp),
        out_shape=(
            jax.ShapeDtypeStruct((rows, rank), BF16),
            jax.ShapeDtypeStruct((rank, cols), F32),
        ),
        grid=(PIECES,),
        in_specs=[
            pl.BlockSpec((rows // PIECES, rank), lambda i: (i, 0)),
            pl.BlockSpec((rank, cols // PIECES), lambda i: (0, i)),
            pl.BlockSpec((rank, rank), lambda i: (0, 0)),
        ],
        out_specs=(
            pl.BlockSpec((rows // PIECES, rank), lambda i: (i, 0)),
            pl.BlockSpec((rank, cols // PIECES), lambda i: (0, i)),
        ),
        cost_estimate=pl.CostEstimate(
            flops=4 * rank * rank * (rows + cols), bytes_accessed=4 * rank * (rows + cols),
            transcendentals=0,
        ),
    )(sk, x, inv)


def solution(mesh):
    return jax.shard_map(
        functools.partial(local, mesh.shape["slot"], mesh.shape["space"]),
        mesh=mesh,
        in_specs=(
            P("space", "slot"),
            P("space", "slot"),
            P("space", "slot"),
            P("space", "slot"),
            P("slot", None),
            P(),
            P(),
        ),
        out_specs=(P("space", None), P(None, "slot")),
        check_vma=False,
    )
```

```python
import functools

import jax
import jax.numpy as jnp
from jax import lax
from jax.experimental import pallas as pl
from jax.experimental.pallas import tpu as pltpu
from jax.sharding import PartitionSpec as P

MESH = pl.DeviceIdType.MESH
F32, BF16 = jnp.float32, jnp.bfloat16
SUB = 4
PIECES = 4
WIDE = 16


def dot(a, b, contract=((1,), (0,))):
    return lax.dot_general(a, b, (contract, ((), ())), preferred_element_type=F32)


def dot_full(a, b, contract=((1,), (0,))):
    return lax.dot_general(
        a, b, (contract, ((), ())), precision=lax.Precision.HIGHEST, preferred_element_type=F32
    )


def split(x):
    hi = x.astype(BF16)
    return hi, (x - hi.astype(F32)).astype(BF16)


def inverse_lower(t_ref, size, between):
    row = lax.broadcasted_iota(jnp.int32, (size, size), 0)
    lane = lax.broadcasted_iota(jnp.int32, (size, size), 1)
    sub = lax.broadcasted_iota(jnp.int32, (WIDE, size), 0)
    lane_t = lax.broadcasted_iota(jnp.int32, (WIDE, size), 1)
    lane1 = lax.broadcasted_iota(jnp.int32, (1, size), 1)

    def round_of(g, _):
        rest = t_ref[WIDE:, :]
        tile = t_ref[:WIDE, :]
        cols = [jnp.broadcast_to(tile[:, j : j + 1], (WIDE, size)) for j in range(WIDE)]
        inv_t = jnp.zeros((WIDE, size), F32)
        for s in range(WIDE):
            inv = 1.0 / cols[s][s : s + 1, :]
            inv_t = jnp.where(sub == s, inv, inv_t)
            m = jnp.where(sub > s, cols[s], 0.0) * inv
            r = jnp.where(lane1 == s, 1.0, tile[s : s + 1, :])
            for j in range(s + 1, WIDE):
                cols[j] = cols[j] - m * cols[j][s : s + 1, :]
            tile = jnp.where((sub > s) & (lane_t == s), 0.0, tile) - m * r
        left = size - WIDE * g
        mult = jnp.where((lane_t >= WIDE) & (lane_t < left), tile * inv_t, 0.0)
        unit = jnp.where(lane_t < sub, tile, jnp.where(lane_t == sub, 1.0, 0.0))
        rows = jnp.where(lane_t < WIDE, unit, tile)
        change = dot_full(mult, rows, ((0,), (0,)))
        open_rows = (row[WIDE:] < left) & (lane[WIDE:] < WIDE)
        rest = jnp.where(open_rows, 0.0, rest) - change[WIDE:]
        t_ref[: size - WIDE, :] = pltpu.roll(rest, size - WIDE, 1)
        t_ref[size - WIDE :, :] = pltpu.roll(tile, size - WIDE, 1)
        return 0

    done, rounds = 0, size // WIDE
    for at, action in between:
        at = min(int(at * rounds), rounds)
        lax.fori_loop(done, at, round_of, 0)
        action()
        done = at
    lax.fori_loop(done, rounds, round_of, 0)
    t = t_ref[...]
    pivot = jnp.sum(jnp.where(row == lane, t, 0.0), axis=1, keepdims=True)
    unit = jnp.where(row > lane, t, jnp.where(row == lane, 1.0, 0.0))
    return unit * lax.rsqrt(pivot)


def kernel(
    n, nsp,
    vals, scales, slab, slab_sc, test, owner, offset,
    sk_o, x_o, inv_ref,
    vbuf, win, win_s, msc, place, tm_out, tm_in, part, rs_out, rs_in, sk, skt,
    gr, g_out, g_in, g_fin, cr, c_out, c_in, c_fin, sl_in, t_ref, gpart,
    tm_ss, tm_rs, rr_ss, rr_rs, rl_ss, rl_rs, ar_ss, ar_rs, al_ss, al_rs,
    g_ss, g_rs, c_ss, c_rs, sl_ss, sl_rs, v_sem, o_sem,
):
    z = lax.axis_index("slot")
    me = lax.axis_index("space")
    core = lax.rem(me, 2)
    rows, cols = vals.shape
    rank = test.shape[1]
    block = rows // scales.shape[0]
    sc = slab.shape[1]
    sw = sl_in.shape[2]
    nb = nsp.bit_length() - 1
    half = rank // 2
    chunk = rows // n
    sub = chunk // SUB
    total_rows = rows * nsp

    strides = [jnp.int32(1)]
    for i in range(1, nb):
        strides.append((1 << i) * (1 - core) + (1 << (nb - i)) * core)
    strides.append(jnp.int32(1))

    def partner(stride):
        return me + stride * (1 - 2 * lax.rem(me // stride, 2))

    def copy(src, dst, ss, rs, space=None, slot=None):
        return pltpu.make_async_remote_copy(
            src_ref=src, dst_ref=dst, send_sem=ss, recv_sem=rs,
            device_id={"space": me if space is None else space, "slot": z if slot is None else slot},
            device_id_type=MESH,
        )

    def load(c):
        at = pl.ds(pl.multiple_of(c * chunk, chunk), chunk)
        return pltpu.make_async_copy(vals.at[at], vbuf.at[at], v_sem.at[c])

    for c in range(n):
        load(c).start()

    barrier = pltpu.get_barrier_semaphore()
    for d in range(1, n):
        pl.semaphore_signal(
            barrier, inc=1, device_id={"space": me, "slot": lax.rem(z + d, n)}, device_id_type=MESH
        )
    for i in range(nb):
        pl.semaphore_signal(
            barrier, inc=1, device_id={"space": partner(jnp.int32(1 << i)), "slot": z}, device_id_type=MESH
        )

    first = jnp.where(owner[0] == z, offset[0], -(2 ** 20))

    @pl.loop(0, n)
    def _(s):
        diff = lax.broadcasted_iota(jnp.int32, (sc, cols), 1) - lax.broadcasted_iota(
            jnp.int32, (sc, cols), 0
        )
        one_hot = jnp.where(diff == first + s * sc, 1.0, 0.0).astype(BF16)
        place[pl.ds(pl.multiple_of(s * sc, sc), sc), :] = one_hot
        tm_out[s] = dot(one_hot, test[...]).astype(BF16)

    pl.semaphore_wait(barrier, n - 1 + nb)

    def tm_copy(d):
        peer = lax.rem(z + d, n)
        return copy(tm_out.at[peer], tm_in.at[d], tm_ss.at[d], tm_rs.at[d], slot=peer)

    for d in range(1, n):
        tm_copy(d).start()

    col = lax.broadcasted_iota(jnp.int32, scales.shape, 1) - first
    replaced = (col >= 0) & (col < n * sc)
    msc[...] = jnp.where(replaced, 0.0, scales[...].astype(F32))

    ssc = slab_sc[...].astype(F32)
    for b in range(rows // block):
        win_s[b * block : (b + 1) * block, :] = (
            slab[b * block : (b + 1) * block, :].astype(F32) * ssc[b : b + 1, :]
        ).astype(BF16)

    @pl.loop(0, n)
    def _(c):
        load(c).wait()

        @pl.loop(0, chunk // block)
        def _(i):
            b = c * (chunk // block) + i
            at = pl.ds(pl.multiple_of(b * block, block), block)
            w = (vbuf[at, :].astype(F32) * msc[pl.ds(b, 1), :]).astype(BF16)
            win[at, :] = w
            part[at, :] = dot(w, test[...])

    rows_new = tm_out[z].astype(F32)
    for d in range(1, n):
        tm_copy(d).wait_recv()
        rows_new += tm_in[d].astype(F32)
    rows_new = rows_new.astype(BF16)

    def add_new(c):
        at = pl.ds(pl.multiple_of(c * chunk, chunk), chunk)
        part[at, :] += dot(win_s[at, :], rows_new)

    def span(c, h):
        return pl.ds(pl.multiple_of(c * chunk + h * sub, sub), sub)

    def rs_copy(way, c, h):
        ss, rs = ((rr_ss, rr_rs), (rl_ss, rl_rs))[way]
        step = 1 - 2 * way
        at = span(c, h)
        return copy(
            rs_out.at[way, at], rs_in.at[way, at], ss.at[c, h], rs.at[c, h], slot=z + step
        )

    has = (z > 0, z < n - 1)
    for d in range(n - 1, 0, -1):
        for way in (0, 1):
            c = z + d * (1 - 2 * way)

            @pl.when((c >= 0) & (c < n))
            def _():
                add_new(c)

        for h in range(SUB):
            for way in (0, 1):
                c = z + d * (1 - 2 * way)

                @pl.when((c >= 0) & (c < n))
                def _():
                    at = span(c, h)

                    @pl.when(has[way])
                    def _():
                        rs_copy(way, c, h).wait_recv()
                        part[at, :] += rs_in[way, at, :].astype(F32)

                    rs_out[way, at, :] = part[at, :].astype(BF16)
                    rs_copy(way, c, h).start()

    add_new(z)

    def ag_copy(way, c, h):
        ss, rs = ((ar_ss, ar_rs), (al_ss, al_rs))[way]
        at = span(c, h)
        return copy(sk.at[at], sk.at[at], ss.at[c, h], rs.at[c, h], slot=z + 1 - 2 * way)

    for h in range(SUB):
        at = span(z, h)
        for way in (0, 1):

            @pl.when(has[way])
            def _():
                rs_copy(way, z, h).wait_recv()
                part[at, :] += rs_in[way, at, :].astype(F32)

        sk[at, :] = part[at, :].astype(BF16)
        for way in (0, 1):

            @pl.when(has[1 - way])
            def _():
                ag_copy(way, z, h).start()

    width = 2 * rank if cols % (2 * rank) == 0 else rank
    blocks = cols // width
    cr[...] = jnp.zeros(cr.shape, F32)

    def gram_of(c):
        at = pl.ds(pl.multiple_of(c * chunk, chunk), chunk)
        s = sk[at, :]
        t = s.astype(F32).T.astype(BF16)
        skt[:, at] = t
        gpart[c] = dot(t, s)

    def cross_of(c):
        at = pl.ds(pl.multiple_of(c * chunk, chunk), chunk)
        t = skt[:, at]
        cr[:, cols : cols + sc] += dot(t, win_s[at, :])

        @pl.loop(0, blocks)
        def _(b):
            to = pl.ds(pl.multiple_of(b * width, width), width)
            cr[:, to] += dot(t, win[at, to])

    def at_distance(d, action):
        for c in (z - d, z + d)[: 2 if d else 1]:

            @pl.when((c >= 0) & (c < n))
            def _():
                action(c)

    gram_of(z)
    for d in range(1, n):
        at_distance(d - 1, cross_of)
        for h in range(SUB):
            for way in (0, 1):
                c = z - d * (1 - 2 * way)

                @pl.when((c >= 0) & (c < n))
                def _():
                    ag_copy(way, c, h).wait_recv()

                    @pl.when(has[1 - way])
                    def _():
                        ag_copy(way, c, h).start()

        at_distance(d, gram_of)

    out_sk = pltpu.make_async_copy(sk, sk_o, o_sem.at[0])
    out_sk.start()

    def half_at(c):
        return pl.ds(pl.multiple_of(c * half, half), half)

    def g_copy(i):
        if i == 0:
            return copy(gr.at[half_at(1 - core)], g_in.at[0], g_ss.at[0], g_rs.at[0], space=partner(strides[0]))
        if i < nb:
            return copy(g_out.at[i], g_in.at[i], g_ss.at[i], g_rs.at[i], space=partner(strides[i]))
        at = half_at(core)
        return copy(g_fin.at[at], g_fin.at[at], g_ss.at[i], g_rs.at[i], space=partner(strides[0]))

    def g_step(i):
        own = gr[half_at(core), :] if i == 1 else g_out[i - 1]
        g_copy(i - 1).wait_recv()
        total = own + g_in[i - 1]
        if i < nb:
            g_out[i] = total
        else:
            g_fin[half_at(core), :] = total
        g_copy(i).start()

    total = gpart[0]
    for c in range(1, n):
        total += gpart[c]
    gr[...] = total
    g_copy(0).start()
    at_distance(n - 1, cross_of)

    def c_copy(i):
        if i < nb:
            return copy(c_out.at[i], c_in.at[i], c_ss.at[i], c_rs.at[i], space=partner(strides[i]))
        at = half_at(core)
        return copy(c_fin.at[at], c_fin.at[at], c_ss.at[i], c_rs.at[i], space=partner(strides[0]))

    g_step(1)
    c_out[0] = cr[half_at(1 - core), :].astype(BF16)
    c_copy(0).start()
    for i in range(2, nb):
        g_step(i)

    def c_step(i):
        c_copy(i - 1).wait_recv()
        own = cr[half_at(core), :] if i == 1 else c_out[i - 1].astype(F32)
        total = (own + c_in[i - 1].astype(F32)).astype(BF16)
        if i < nb:
            c_out[i] = total
        else:
            c_fin[half_at(core), :] = total
        c_copy(i).start()

    def sl_copy(d):
        return copy(
            c_fin.at[:, pl.ds(cols, sw)], sl_in.at[d], sl_ss.at[d], sl_rs.at[d], slot=lax.rem(z + d, n)
        )

    def sl_start():
        c_copy(nb).wait_recv()
        for d in range(1, n):
            sl_copy(d).start()

    c_step(1)
    g_step(nb)
    g_copy(nb).wait_recv()

    spots = [
        (0.5 + 0.65 * (i - 2) / (nb - 2), functools.partial(c_step, i)) for i in range(2, nb + 1)
    ] + [(1.4, sl_start)]
    early = [(at, f) for at, f in spots if at < 1]
    late = [(at - 1, f) for at, f in spots if at >= 1]
    scale = 1.0 / total_rows
    t_ref[...] = g_fin[:half, :half] * scale
    inv1 = inverse_lower(t_ref, half, early)
    low = dot_full(g_fin[half:, :half] * scale, inv1, ((1,), (1,)))
    t_ref[...] = g_fin[half:, half:] * scale - dot_full(low, low, ((1,), (1,)))
    inv2 = inverse_lower(t_ref, half, late)
    inv_ref[:half, :half] = inv1
    inv_ref[:half, half:] = jnp.zeros((half, half), F32)
    inv_ref[half:, :half] = -dot_full(inv2, dot_full(low, inv1))
    inv_ref[half:, half:] = inv2

    for d in range(1, n):
        sl_copy(d).wait_recv()

    @pl.loop(0, blocks)
    def _(b):
        at = pl.ds(pl.multiple_of(b * width, width), width)
        x = c_fin[:, at].astype(F32)
        for d in range(n):
            src = lax.rem(z + n - d, n)
            p = place[pl.ds(pl.multiple_of(src * sc, sc), sc), at]
            own = c_fin[:, cols : cols + sc] if d == 0 else sl_in[d, :, :sc]
            x += dot(own, p)
        x_o[:, at] = x.astype(BF16)

    for d in range(1, n):
        tm_copy(d).wait_send()
        sl_copy(d).wait_send()
        for h in range(SUB):
            for way in (0, 1):
                c = z + d * (1 - 2 * way)

                @pl.when((c >= 0) & (c < n))
                def _():
                    rs_copy(way, c, h).wait_send()

    for d in range(n):
        for h in range(SUB):
            for way in (0, 1):
                c = z - d * (1 - 2 * way)

                @pl.when((c >= 0) & (c < n) & has[1 - way])
                def _():
                    ag_copy(way, c, h).wait_send()

    for i in range(nb + 1):
        g_copy(i).wait_send()
        c_copy(i).wait_send()
    out_sk.wait()


def apply(total_rows, sk, x, inv, basis_o, coef_o):
    hi, lo = split(inv[...])
    s = sk[...]
    basis_o[...] = (dot(s, hi, ((1,), (1,))) + dot(s, lo, ((1,), (1,)))).astype(BF16)
    v = x[...]
    coef_o[...] = (dot(hi, v) + dot(lo, v)) * (1.0 / total_rows ** 0.5)


def local(n, nsp, vals, scales, slab, slab_sc, test, owner, offset):
    rows, cols = vals.shape
    rank = test.shape[1]
    sc = slab.shape[1]
    sw = -(-sc // 128) * 128
    nb = nsp.bit_length() - 1
    half = rank // 2
    vmem = pl.BlockSpec(memory_space=pltpu.VMEM)
    smem = pl.BlockSpec(memory_space=pltpu.SMEM)
    dma = pltpu.SemaphoreType.DMA
    flops = 2 * rank * (2 * rows * cols + 3 * rank * rows + 2 * rank * cols)
    sk, x, inv = pl.pallas_call(
        functools.partial(kernel, n, nsp),
        out_shape=(
            jax.ShapeDtypeStruct((rows, rank), BF16),
            jax.ShapeDtypeStruct((rank, cols), BF16),
            jax.ShapeDtypeStruct((rank, rank), F32),
        ),
        in_specs=[pl.BlockSpec(memory_space=pl.ANY)] + [vmem] * 4 + [smem] * 2,
        out_specs=(pl.BlockSpec(memory_space=pl.ANY), vmem, vmem),
        scratch_shapes=[
            pltpu.VMEM((rows, cols), BF16),
            pltpu.VMEM((rows, cols), BF16),
            pltpu.VMEM((rows, sc), BF16),
            pltpu.VMEM(scales.shape, F32),
            pltpu.VMEM((n * sc, cols), BF16),
            pltpu.VMEM((n, sc, rank), BF16),
            pltpu.VMEM((n, sc, rank), BF16),
            pltpu.VMEM((rows, rank), F32),
            pltpu.VMEM((2, rows, rank), BF16),
            pltpu.VMEM((2, rows, rank), BF16),
            pltpu.VMEM((rows, rank), BF16),
            pltpu.VMEM((rank, rows), BF16),
            pltpu.VMEM((rank, rank), F32),
            pltpu.VMEM((nb, half, rank), F32),
            pltpu.VMEM((nb, half, rank), F32),
            pltpu.VMEM((rank, rank), F32),
            pltpu.VMEM((rank, cols + sw), F32),
            pltpu.VMEM((nb, half, cols + sw), BF16),
            pltpu.VMEM((nb, half, cols + sw), BF16),
            pltpu.VMEM((rank, cols + sw), BF16),
            pltpu.VMEM((n, rank, sw), BF16),
            pltpu.VMEM((half, half), F32),
            pltpu.VMEM((n, rank, rank), F32),
            dma((n,)), dma((n,)),
            dma((n, SUB)), dma((n, SUB)), dma((n, SUB)), dma((n, SUB)),
            dma((n, SUB)), dma((n, SUB)), dma((n, SUB)), dma((n, SUB)),
            dma((nb + 1,)), dma((nb + 1,)), dma((nb + 1,)), dma((nb + 1,)),
            dma((n,)), dma((n,)), dma((n,)), dma((1,)),
        ],
        compiler_params=pltpu.CompilerParams(
            collective_id=0, has_side_effects=True, vmem_limit_bytes=60 * 2 ** 20
        ),
        cost_estimate=pl.CostEstimate(
            flops=flops, bytes_accessed=2 * rows * cols + 4 * rank * cols, transcendentals=0
        ),
    )(vals, scales, slab, slab_sc, test, owner, offset)
    return pl.pallas_call(
        functools.partial(apply, rows * nsp),
        out_shape=(
            jax.ShapeDtypeStruct((rows, rank), BF16),
            jax.ShapeDtypeStruct((rank, cols), F32),
        ),
        grid=(PIECES,),
        in_specs=[
            pl.BlockSpec((rows // PIECES, rank), lambda i: (i, 0)),
            pl.BlockSpec((rank, cols // PIECES), lambda i: (0, i)),
            pl.BlockSpec((rank, rank), lambda i: (0, 0)),
        ],
        out_specs=(
            pl.BlockSpec((rows // PIECES, rank), lambda i: (i, 0)),
            pl.BlockSpec((rank, cols // PIECES), lambda i: (0, i)),
        ),
        cost_estimate=pl.CostEstimate(
            flops=4 * rank * rank * (rows + cols), bytes_accessed=4 * rank * (rows + cols),
            transcendentals=0,
        ),
    )(sk, x, inv)


def solution(mesh):
    return jax.shard_map(
        functools.partial(local, mesh.shape["slot"], mesh.shape["space"]),
        mesh=mesh,
        in_specs=(
            P("space", "slot"),
            P("space", "slot"),
            P("space", "slot"),
            P("space", "slot"),
            P("slot", None),
            P(),
            P(),
        ),
        out_specs=(P("space", None), P(None, "slot")),
        check_vma=False,
    )
```
